32 devices in a mesh: ctx: 2 (over x), head: 8 (over z, y), pool: 2 (over core).
Axes of the slice: x: 2, y: 2, z: 4, core: 2. Of those that a mesh axis runs over, the one named last changes fastest.
Arguments:
- queries: bfloat16 [2, 256, 64, 576], P('pool', 'ctx', 'head')
- new_latent: bfloat16 [2, 256, 576], P('pool', 'ctx')
- cache_pool: bfloat16 [2, 32, 64, 576], P('ctx', 'pool'), may hold values from -6 to 6
- block_list: int32 [2, 2, 16], P('pool', 'ctx'), may hold values from 0 to 31, as said below
- cached_lengths: int32 [2], P('pool'), may hold values from 682 to 2048
- w_uv: bfloat16 [64, 512, 128], P('head'), may hold values from -4 to 4
- w_o: bfloat16 [64, 128, 7168], P('head'), may hold values from -0.09375 to 0.09375
Outputs:
- mixed: bfloat16 [2, 256, 7168], P('pool', 'ctx', 'head')
The draws below stay inside these ranges and needn't reach their ends.
Inputs may be any that keep to these rules, and one draw needn't show every extreme that they name: For each ctx index c, block_list[:, c, :] holds every slot 0 to 31 exactly once.
All inputs are finite; a program needn't handle non-finite values.
Results may differ from the reference program's by a relative error of at most 0.015.
Values may be sent and summed in bfloat16 or wider, within the bound.
No kernel may reach another device: no remote copies, remote signals or barrier semaphores. Data moves between devices by JAX's collectives and lax.ppermute only.
A program may use at most 64 MiB of HBM per device.

```python
import jax
import jax.numpy as jnp
from jax import lax

D = 7168
HEADS = 64
LAT = 512
ROPE = 64
VH = 128
BLK = 64
NEWDEV = 128
HB = 16
CONVS = 2
NEW = 256
HIST = 2048
SLOTS = 32
N_CTX = 2


def shared_latent(key):
    base = jax.random.normal(jax.random.fold_in(key, 1), (CONVS, NEW, LAT + ROPE), jnp.float32)
    return base


def draw_new_latent(key, part):
    base = shared_latent(key)
    latent = base
    return latent.astype(jnp.bfloat16)


def draw_queries(key, part):
    key = jax.random.fold_in(key, 22)
    shape_q = (CONVS, NEW, HEADS, LAT + ROPE)
    query_vals = jax.random.normal(key, shape_q, jnp.float32)
    return query_vals.astype(jnp.bfloat16)


def draw_block_list(key, part):
    key = jax.random.fold_in(key, 11)
    cycle_size = NEW // NEWDEV
    cycle_keys = jax.random.split(key, cycle_size)
    orders = jax.vmap(lambda one_key: jax.random.permutation(one_key, SLOTS))(cycle_keys)
    orders = orders.astype(jnp.int32).reshape(cycle_size, CONVS, HB)
    return jnp.transpose(orders, (1, 0, 2))


def draw_cached_lengths(key, part):
    key = jax.random.fold_in(key, 12)
    longest = jax.random.randint(jax.random.fold_in(key, 1), (), 0, CONVS)
    others = jax.random.randint(jax.random.fold_in(key, 2), (CONVS,), HIST // 3, HIST + 1)
    conv_ids = jnp.arange(CONVS, dtype=jnp.int32)
    return jnp.where(conv_ids == longest, HIST, others).astype(jnp.int32)


def with_spikes(values, own_key, source, target, parts, factor):
    owner, partner = [(jnp.arange(values.shape[axis_at]) // (values.shape[axis_at] // parts)).reshape([-1 if axis == axis_at else 1 for axis in range(values.ndim)]) for axis_at in (source, target)]
    chosen = jax.random.permutation(own_key, parts)[partner]
    strong = (owner == chosen) | (owner == (partner + parts // 2) % parts)
    return jnp.where(strong, factor * values, values)


def shard_levels(stream_key, shape, pieces, least, high):
    def one(dim, shards_of):
        heights = jax.random.uniform(jax.random.fold_in(jax.random.fold_in(stream_key, 6), dim), (shards_of,), jnp.float32, least / len(pieces), high / len(pieces))
        return jnp.repeat(jnp.exp(heights), shape[dim] // shards_of).reshape((-1,) + (1,) * (len(shape) - dim - 1))

    factor_of = one(*pieces[0])
    for cut in pieces[1:]:
        factor_of = factor_of * one(*cut)
    return factor_of


def centred(rng, dims, scale, bound, cuts=(), kind=jnp.bfloat16):
    entries = scale * jax.random.normal(rng, dims, jnp.float32)
    if cuts:
        entries = entries * shard_levels(rng, dims, cuts, -0.22, 0.18)
    return jnp.clip(entries, -bound, bound).astype(kind)


def heavy_noise(key, extent, width, limit, cuts, heavy, kind=jnp.bfloat16):
    values = width * jax.random.normal(key, extent, jnp.float32)
    if cuts:
        values = values * shard_levels(key, extent, cuts, -0.22, 0.18)
    return jnp.clip(with_spikes(values, jax.random.fold_in(key, 3), *heavy), -limit, limit).astype(kind)


def setup_inputs(seed: int = 0) -> dict:
    splits = jax.random.split(jax.random.key(seed), 8)
    return {
        "queries": draw_queries(jax.random.fold_in(splits[7], 71), 0),
        "new_latent": draw_new_latent(jax.random.fold_in(splits[7], 71), 0),
        "cache_pool": centred(splits[2], (N_CTX, SLOTS, BLK, LAT + ROPE), 1.0, 6.0, ((0, 2), (1, 2))),
        "block_list": draw_block_list(jax.random.fold_in(splits[7], 71), 0),
        "cached_lengths": draw_cached_lengths(jax.random.fold_in(splits[7], 71), 0),
        "w_uv": centred(splits[5], (HEADS, LAT, VH), 0.25, 4.0, ((0, 8),)),
        "w_o": heavy_noise(splits[6], (HEADS, VH, D), (HEADS * VH) ** -0.5, 0.09375, ((0, 8),), (0, 2, 8, 2.0)),
    }


score_scale = 192.0 ** -0.5
neg_big = -1e30


def one_conversation(query_conv, latent_conv, cache_pool, blocks_conv, cached):
    cycle_ids = jnp.arange(cache_pool.shape[0], dtype=jnp.int32)
    history = cache_pool[cycle_ids[:, None], blocks_conv]
    history = history.reshape(HIST, LAT + ROPE)
    key_latent = jnp.concatenate([history, latent_conv], axis=0)
    key_rows = jnp.arange(HIST + NEW, dtype=jnp.int32)
    query_rows = jnp.arange(NEW, dtype=jnp.int32)
    visible = jnp.where((key_rows < HIST)[None, :], (key_rows < cached)[None, :],
                        (key_rows - HIST)[None, :] <= query_rows[:, None])
    value_part = key_latent[:, :LAT].astype(jnp.float32)

    def per_head(query_head):
        scores = jnp.dot(query_head, key_latent.T, preferred_element_type=jnp.float32) * score_scale
        scores = jnp.where(visible, scores, neg_big)
        row_max = jnp.max(scores, axis=1, keepdims=True)
        weights = jnp.where(visible, jnp.exp(scores - row_max), 0.0)
        denominator = jnp.sum(weights, axis=1, keepdims=True)
        latent_out = jnp.dot(weights, value_part, preferred_element_type=jnp.float32) / denominator
        return latent_out.astype(jnp.bfloat16)

    latent_out = lax.map(per_head, jnp.transpose(query_conv, (1, 0, 2)))
    return latent_out


def reference(queries, new_latent, cache_pool, block_list, cached_lengths, w_uv, w_o):
    results = []
    for conv_index in range(CONVS):
        latent_out = one_conversation(queries[conv_index], new_latent[conv_index], cache_pool,
                                      block_list[conv_index], cached_lengths[conv_index])
        head_out = jnp.einsum('hnl,hlv->nhv', latent_out.astype(jnp.float32), w_uv.astype(jnp.float32))
        head_out = head_out.astype(jnp.bfloat16)
        mixed_conv = jnp.dot(head_out.reshape(NEW, HEADS * VH), w_o.reshape(HEADS * VH, D),
                             preferred_element_type=jnp.float32)
        results.append(mixed_conv.astype(jnp.bfloat16))
    return jnp.stack(results, axis=0)
```

```python
import functools

import jax
import jax.numpy as jnp
from jax import lax
from jax.experimental import pallas as pl
from jax.experimental.pallas import tpu as pltpu
from jax.sharding import PartitionSpec as P

score_scale = 192.0 ** (-0.5)
log2_e = 1.4426950408889634
exp2_scale = score_scale * log2_e
neg_big = -1e30
pos_big = 3e38
LANES = 128
CHUNK = 64
ANY_SPEC = pl.BlockSpec(memory_space=pl.ANY)
HBM_SPEC = pl.BlockSpec(memory_space=pltpu.HBM)
VMEM_SPEC = pl.BlockSpec(memory_space=pltpu.VMEM)
SMEM_SPEC = pl.BlockSpec(memory_space=pltpu.SMEM)


def slot_order(order):
    bits = len(order)
    return [
        sum(((rank >> (bits - 1 - i)) & 1) << order[i] for i in range(bits))
        for rank in range(1 << bits)
    ]


def in_vmem(shape, dtype=jnp.bfloat16):
    return pltpu.VMEM(shape, dtype)


def pin(value, space):
    return pltpu.with_memory_space_constraint(value, space)


def fetch_block(listed, k, own, core, target, sem):
    slots = own.shape[0]
    slot = listed[k]
    place = slot & (slots - 1)
    here = slot // slots == lax.axis_index("pool")

    @pl.when(here)
    def _():
        pltpu.make_async_copy(own.at[place], target, sem).start()

    @pl.when(jnp.logical_not(here))
    def _():
        pltpu.make_async_copy(core.at[place], target, sem).start()


def pick_kernel(quarter, listed, own, core, first, sem):
    blk = own.shape[1]
    lead = quarter * (lax.axis_index("head") & 3)
    for j in range(quarter):
        fetch_block(listed, lead + j, own, core, first.at[pl.ds(j * blk, blk)], sem.at[0])
    pltpu.make_async_copy(first, first, sem.at[0]).wait()


def pick_quarter(listed, own, core, quarter):
    _, blk, width = own.shape
    return pl.pallas_call(
        functools.partial(pick_kernel, quarter),
        out_shape=in_vmem((quarter * blk, width)),
        in_specs=[SMEM_SPEC, HBM_SPEC, VMEM_SPEC],
        out_specs=VMEM_SPEC,
        scratch_shapes=[pltpu.SemaphoreType.DMA((1,))],
        compiler_params=pltpu.CompilerParams(vmem_limit_bytes=4 << 20),
        cost_estimate=pl.CostEstimate(
            flops=0, bytes_accessed=4 * quarter * blk * width, transcendentals=0
        ),
        name="pick_quarter",
    )(pin(listed, pltpu.SMEM), pin(own, pltpu.HBM), pin(core, pltpu.VMEM))


def attend_kernel(cfg, *refs):
    pieces, first, last, heads, tokens, lat, direct_rows, items = cfg
    refs = list(refs)
    take = lambda n: [refs.pop(0) for _ in range(n)]
    (cached,) = take(1)
    if first:
        listed, own, core = take(3)
    (q,) = take(1)
    bufs = take(len(pieces) - first)
    state_in = [] if first else take(3)
    if last:
        uv, wo_hbm = take(2)
        ho_out, *sent = take(1 + len({part for part, *_ in items}))
    else:
        acc, m_ref, l_ref = take(3)
        if first:
            (direct,) = take(1)
    kv, vt, cap, s_buf, p_buf, sems = take(6)
    if last:
        ho_t, *weights = refs
    pairs = heads // 2
    keys = kv.shape[0]

    if first:
        blk = own.shape[1]
        for k in range(pieces[0][0] // blk):
            fetch_block(listed, k, own, core, kv.at[pl.ds(k * blk, blk)], sems.at[0])
    weight_copies = start_weights(items, wo_hbm, weights, sems) if last else []

    at = 0
    for i, (rows, is_new, limit_of) in enumerate(pieces):
        limit = limit_of(cached[0])
        row = lax.broadcasted_iota(jnp.int32, (rows, tokens), 0)
        if is_new:
            limit = lax.broadcasted_iota(jnp.int32, (rows, tokens), 1) + 1 + limit
        cap[pl.ds(at, rows), :] = jnp.where(row < limit, pos_big, neg_big)
        if i >= first:
            kv[pl.ds(at, rows), :] = bufs[i - first][...]
        at += rows
    if first:
        fetched = kv.at[pl.ds(0, pieces[0][0])]
        pltpu.make_async_copy(fetched, fetched, sems.at[0]).wait()
        direct[...] = kv[pieces[0][0] - direct_rows : pieces[0][0], :]

    def scores(i):
        q_pair = jnp.concatenate([q[2 * i], q[2 * i + 1]], axis=1)
        s_buf[i % 2] = jnp.dot(kv[...], q_pair, preferred_element_type=jnp.float32)

    def fold(x):
        return x.reshape(CHUNK // 8, 8, x.shape[1])

    scores(0)
    vt[...] = kv[:, :lat].T
    for i in range(pairs):
        if i + 1 < pairs:
            scores(i + 1)
        buf, weight = s_buf.at[i % 2], p_buf.at[i % 2]
        top = jnp.full((8, 2 * tokens), -jnp.inf, jnp.float32)
        for r in range(0, keys, CHUNK):
            limits = cap[r : r + CHUNK, :]
            x = jnp.minimum(buf[r : r + CHUNK, :], jnp.concatenate([limits, limits], axis=1))
            buf[r : r + CHUNK, :] = x
            top = jnp.maximum(top, jnp.max(fold(x), axis=0))
        m = jnp.max(top, axis=0, keepdims=True)
        if not first:
            m_old, l_old, acc_old = [ref[i] for ref in state_in]
            m = jnp.maximum(m, m_old)
        scaled = m * exp2_scale
        total = jnp.zeros((8, 2 * tokens), jnp.float32)
        for r in range(0, keys, CHUNK):
            p = jnp.exp2(buf[r : r + CHUNK, :] * exp2_scale - scaled)
            total = total + jnp.sum(fold(p), axis=0)
            weight[r : r + CHUNK, :] = p.astype(jnp.bfloat16)
        l = jnp.sum(total, axis=0, keepdims=True)
        o = jnp.dot(vt[...], weight[...], preferred_element_type=jnp.float32)
        if not first:
            factor = jnp.exp2(m_old * exp2_scale - scaled)
            l = l + l_old * factor
            o = o + acc_old * factor
        if not last:
            m_ref[i] = m
            l_ref[i] = l
            acc[i] = o
            continue
        latent = (o / l).astype(jnp.bfloat16)
        vh = uv.shape[1]
        for k in range(2):
            head = 2 * i + k
            out = jnp.dot(
                uv[head],
                latent[:, k * tokens : (k + 1) * tokens],
                preferred_element_type=jnp.float32,
            )
            ho_t[pl.ds(head * vh, vh), :] = out.astype(jnp.bfloat16)
    if last:
        ho_out[...] = ho_t[...].T
        project_items(items, ho_out, weight_copies, weights, sent)


def start_weights(items, wo_hbm, weights, sems):
    copies = []
    me = lax.axis_index("head")
    for n, (_, j, lo, width) in enumerate(items):
        cols = wo_hbm.shape[1] // lax.axis_size("head")
        start = pl.multiple_of((me ^ j) * cols + lo, LANES)
        copies.append(
            pltpu.make_async_copy(wo_hbm.at[:, pl.ds(start, width)], weights[n], sems.at[1 + n])
        )
        copies[-1].start()
    return copies


def project_items(items, head_out, copies, weights, outs):
    parts = sorted({part for part, *_ in items})
    filled = dict.fromkeys(parts, 0)
    for n, (part, _, _, _) in enumerate(items):
        copies[n].wait()
        value = jnp.dot(head_out[...], weights[n][...], preferred_element_type=jnp.float32)
        outs[parts.index(part)][filled[part]] = value.astype(jnp.bfloat16)
        filled[part] += 1


def item_shapes(items, tokens):
    sizes = {}
    for part, _, _, size in items:
        sizes[part] = (sizes.get(part, (0, size))[0] + 1, size)
    return [in_vmem((sizes[part][0], tokens, sizes[part][1])) for part in sorted(sizes)]


def attend(pieces, cached, q_t, bufs, state, lat, gather=None, last=None):
    heads, width, tokens = q_t.shape
    first = state is None
    items = last[2] if last else ()
    keys = sum(rows for rows, *_ in pieces)
    pairs = heads // 2
    stat = (pairs, 1, 2 * tokens)
    vmem = [q_t, *bufs, *(state or ())]
    flops = 2 * heads * tokens * keys * (width + lat)
    moved = 2 * keys * width
    inputs, specs = [pin(cached, pltpu.SMEM)], [SMEM_SPEC]
    direct_rows = 0
    if first:
        listed, own, core, direct_rows = gather
        inputs += [pin(listed, pltpu.SMEM), pin(own, pltpu.HBM), pin(core, pltpu.VMEM)]
        specs += [SMEM_SPEC, HBM_SPEC, VMEM_SPEC]
    inputs += [pin(value, pltpu.VMEM) for value in vmem]
    specs += [VMEM_SPEC] * len(vmem)
    scratch = [
        pltpu.VMEM((keys, width), jnp.bfloat16),
        pltpu.VMEM((lat, keys), jnp.bfloat16),
        pltpu.VMEM((keys, tokens), jnp.float32),
        pltpu.VMEM((2, keys, 2 * tokens), jnp.float32),
        pltpu.VMEM((2, keys, 2 * tokens), jnp.bfloat16),
        pltpu.SemaphoreType.DMA((1 + len(items),)),
    ]
    if last:
        up, proj, _ = last
        inputs += [pin(up, pltpu.VMEM), pin(proj, pltpu.HBM)]
        specs += [VMEM_SPEC, HBM_SPEC]
        out_shape = [in_vmem((tokens, heads * up.shape[1])), *item_shapes(items, tokens)]
        scratch.append(pltpu.VMEM((heads * up.shape[1], tokens), jnp.bfloat16))
        for _, _, _, size in items:
            scratch.append(pltpu.VMEM((proj.shape[0], size), jnp.bfloat16))
            flops += 2 * tokens * proj.shape[0] * size
            moved += 2 * proj.shape[0] * size
    else:
        out_shape = [
            in_vmem((pairs, lat, 2 * tokens), jnp.float32),
            in_vmem(stat, jnp.float32),
            in_vmem(stat, jnp.float32),
        ]
        if first:
            out_shape.append(in_vmem((direct_rows, width)))
    cfg = (pieces, first, bool(last), heads, tokens, lat, direct_rows, items)
    outs = pl.pallas_call(
        functools.partial(attend_kernel, cfg),
        out_shape=out_shape,
        in_specs=specs,
        out_specs=[VMEM_SPEC] * len(out_shape),
        scratch_shapes=scratch,
        compiler_params=pltpu.CompilerParams(vmem_limit_bytes=24 << 20),
        cost_estimate=pl.CostEstimate(
            flops=flops, bytes_accessed=moved, transcendentals=heads * tokens * keys
        ),
        name="attend_last" if last else "attend_own" if first else "attend_far",
    )(*inputs)
    return outs if last else ((outs[1], outs[2], outs[0]), *outs[3:])


def project_kernel(items, head_out, wo_hbm, *refs):
    parts = len({part for part, *_ in items})
    outs, (sems, *weights) = refs[:parts], refs[parts:]
    copies = start_weights(items, wo_hbm, weights, sems)
    project_items(items, head_out, copies, weights, outs)


def project(head_out, proj, items, name):
    tokens, depth = head_out.shape
    out_shape = item_shapes(items, tokens)
    columns = sum(size for _, _, _, size in items)
    return pl.pallas_call(
        functools.partial(project_kernel, items),
        out_shape=out_shape,
        in_specs=[VMEM_SPEC, HBM_SPEC],
        out_specs=[VMEM_SPEC] * len(out_shape),
        scratch_shapes=[pltpu.SemaphoreType.DMA((1 + len(items),))]
        + [pltpu.VMEM((depth, size), jnp.bfloat16) for _, _, _, size in items],
        compiler_params=pltpu.CompilerParams(vmem_limit_bytes=16 << 20),
        cost_estimate=pl.CostEstimate(
            flops=2 * tokens * depth * columns, bytes_accessed=2 * depth * columns, transcendentals=0
        ),
        name=name,
    )(pin(head_out, pltpu.VMEM), pin(proj, pltpu.HBM))


def flip_bit(value, axis, bit):
    size = lax.axis_size(axis)
    return lax.ppermute(value, axis, [(i, i ^ (1 << bit)) for i in range(size)])


def from_ahead(value, steps):
    size = lax.axis_size("ctx")
    return lax.ppermute(value, "ctx", [((i + steps) % size, i) for i in range(size)])


def add_halves(a, b):
    return (a.astype(jnp.float32) + b.astype(jnp.float32)).astype(jnp.bfloat16)


def sum_to_owner(keep, send, order):
    for stage, bit in enumerate(order):
        got = flip_bit(send, "head", bit)
        if stage + 1 == len(order):
            return keep[0].astype(jnp.float32) + got[0].astype(jnp.float32)
        half = keep.shape[0] // 2
        send = add_halves(keep[half:], got[half:])
        keep = add_halves(keep[:half], got[:half])


def tie(*values):
    return lax.optimization_barrier(values)


def body(queries, new_latent, cache_pool, block_list, cached_lengths, w_uv, w_o):
    n_ctx = lax.axis_size("ctx")
    n_head = lax.axis_size("head")
    own = cache_pool[0]
    listed = block_list[0, 0]
    slots, blk, width = own.shape
    tokens = queries.shape[1]
    lat = w_uv.shape[1]
    blocks = block_list.shape[2]
    hist = blocks * blk
    quarter = 3 * blocks // 16
    rows = quarter * blk
    direct_rows = hist - 4 * rows
    new_own = new_latent[0]
    proj = w_o.reshape(w_o.shape[0] * w_o.shape[1], w_o.shape[2])
    q_t = jnp.transpose(queries[0], (1, 2, 0))
    cols = proj.shape[1] // n_head

    def source_of(step):
        return lax.rem(lax.axis_index("ctx") + step, n_ctx)

    def history_limit(step, first_row):
        return lambda cached: (
            cached - source_of(step) * hist - first_row(lax.axis_index("head") & 3)
        )

    def new_limit(step):
        return lambda cached: (lax.axis_index("ctx") - source_of(step)) * tokens

    core = flip_bit(own, "pool", 0)
    far_new = [from_ahead(new_own, step) for step in range(1, n_ctx)]
    up = jnp.transpose(w_uv, (0, 2, 1))

    first = pick_quarter(listed, own, core, quarter)
    first, *far_new = tie(first, *far_new)
    by_x = from_ahead(first, 1)
    pieces = [(hist, False, history_limit(0, lambda lead: 0))]
    pieces += [(tokens, True, new_limit(step)) for step in range(n_ctx)]
    state, direct = attend(
        tuple(pieces), cached_lengths, q_t, [new_own, *far_new], None, lat,
        gather=(listed, own, core, direct_rows),
    )
    by_x, direct, *state = tie(by_x, direct, *state)

    bits = n_head.bit_length() - 1
    half = n_head // 2
    if cols % LANES == 0 and n_head == 8:
        wide = -(-cols // (2 * LANES)) * LANES
        orders = (tuple(range(bits)), (1, 0) + tuple(range(2, bits)))
        spans = ((0, wide), (wide, cols - wide))
        ranked = [
            [(part, j, *spans[part]) for j in slot_order(order)] for part, order in enumerate(orders)
        ]
        sends = tuple(ranked[0][half:] + ranked[1][half:])
        keeps = tuple(ranked[0][:half] + ranked[1][:half])
    else:
        orders, sends = (), ()

    for step in range(1, n_ctx):
        if step > 1:
            by_x = from_ahead(first, step)
        by_y = flip_bit(by_x, "head", 0)
        by_z = flip_bit(by_x, "head", 1)
        far = from_ahead(direct, step)
        by_zy = flip_bit(by_z[: rows // 2], "head", 0)
        by_yz = flip_bit(by_y[rows // 2 :], "head", 1)
        pieces = tuple(
            (rows, False, history_limit(step, lambda lead, flip=flip: rows * (lead ^ flip)))
            for flip in range(3)
        )
        (state,) = attend(pieces, cached_lengths, q_t, [by_x, by_y, by_z], state, lat)
        pieces = (
            (rows // 2, False, history_limit(step, lambda lead: rows * (lead ^ 3))),
            (rows // 2, False, history_limit(step, lambda lead: rows * (lead ^ 3) + rows // 2)),
            (direct_rows, False, history_limit(step, lambda lead: 4 * rows)),
        )
        if step + 1 < n_ctx:
            (state,) = attend(pieces, cached_lengths, q_t, [by_zy, by_yz, far], state, lat)
    head_out, *sent = attend(
        pieces, cached_lengths, q_t, [by_zy, by_yz, far], state, lat, last=(up, proj, sends)
    )
    if orders:
        kept = project(head_out, proj, keeps, "project_kept")
        done = [sum_to_owner(k, s, order) for k, s, order in zip(kept, sent, orders)]
        return jnp.concatenate(done, axis=1).astype(jnp.bfloat16)[None]
    partial_out = jnp.dot(head_out, proj, preferred_element_type=jnp.float32)
    blocks = jnp.transpose(partial_out.reshape(tokens, n_head, cols), (1, 0, 2)).astype(jnp.bfloat16)
    order = tuple(range(bits))
    mine = lax.axis_index("head") ^ jnp.array(slot_order(order), jnp.int32)
    blocks = jnp.take(blocks, mine, axis=0)
    return sum_to_owner(blocks[:half], blocks[half:], order).astype(jnp.bfloat16)[None]


def solution(mesh):
    in_specs = (
        P("pool", "ctx", "head", None),
        P("pool", "ctx", None),
        P("ctx", "pool", None, None),
        P("pool", "ctx", None),
        P("pool"),
        P("head", None, None),
        P("head", None, None),
    )
    out_specs = P("pool", "ctx", "head")
    return jax.shard_map(body, mesh=mesh, in_specs=in_specs, out_specs=out_specs, check_vma=False)
```

```python
import functools

import jax
import jax.numpy as jnp
from jax import lax
from jax.experimental import pallas as pl
from jax.experimental.pallas import tpu as pltpu
from jax.sharding import PartitionSpec as P

score_scale = 192.0 ** (-0.5)
log2_e = 1.4426950408889634
exp2_scale = score_scale * log2_e
neg_big = -1e30
pos_big = 3e38
LANES = 128
CHUNK = 96
ANY_SPEC = pl.BlockSpec(memory_space=pl.ANY)
HBM_SPEC = pl.BlockSpec(memory_space=pltpu.HBM)
VMEM_SPEC = pl.BlockSpec(memory_space=pltpu.VMEM)
SMEM_SPEC = pl.BlockSpec(memory_space=pltpu.SMEM)


def slot_order(order):
    bits = len(order)
    return [
        sum(((rank >> (bits - 1 - i)) & 1) << order[i] for i in range(bits))
        for rank in range(1 << bits)
    ]


def in_vmem(shape, dtype=jnp.bfloat16):
    return pltpu.VMEM(shape, dtype)


def pin(value, space):
    return pltpu.with_memory_space_constraint(value, space)


def fetch_block(listed, k, own, core, target, sem):
    slots = own.shape[0]
    slot = listed[k]
    place = slot & (slots - 1)
    here = (slot >= 0) & (slot < slots)

    @pl.when(here)
    def _():
        pltpu.make_async_copy(own.at[place], target, sem).start()

    @pl.when(jnp.logical_not(here))
    def _():
        pltpu.make_async_copy(core.at[place], target, sem).start()


def quarter_of(flip):
    return (lax.axis_index("head") & 3) ^ flip


def pick_kernel(quarter, listed, own, core, new, piece, sem):
    blk = own.shape[1]
    part = new.shape[0] // 4
    for j in range(quarter):
        target = piece.at[pl.ds(j * blk, blk)]
        fetch_block(listed, quarter * quarter_of(0) + j, own, core, target, sem.at[0])
    rows = pl.ds(pl.multiple_of(quarter_of(0) * part, part), part)
    piece[pl.ds(quarter * blk, part), :] = new[rows, :]
    fetched = piece.at[pl.ds(0, quarter * blk)]
    pltpu.make_async_copy(fetched, fetched, sem.at[0]).wait()


def pick_quarter(listed, own, core, new, quarter):
    _, blk, width = own.shape
    return pl.pallas_call(
        functools.partial(pick_kernel, quarter),
        out_shape=in_vmem((quarter * blk + new.shape[0] // 4, width)),
        in_specs=[SMEM_SPEC, HBM_SPEC, VMEM_SPEC, VMEM_SPEC],
        out_specs=VMEM_SPEC,
        scratch_shapes=[pltpu.SemaphoreType.DMA((1,))],
        compiler_params=pltpu.CompilerParams(vmem_limit_bytes=4 << 20),
        cost_estimate=pl.CostEstimate(
            flops=0, bytes_accessed=4 * quarter * blk * width, transcendentals=0
        ),
        name="pick_quarter",
    )(listed, pin(own, pltpu.HBM), pin(core, pltpu.VMEM), pin(new, pltpu.VMEM))


def attend_kernel(cfg, *refs):
    spans, sizes, pairs, groups, gather, turn, last, tokens, lat, items = cfg
    refs = list(refs)
    take = lambda n: [refs.pop(0) for _ in range(n)]
    (cached,) = take(1)
    listed, own, core = take(3) if gather else (None, None, None)
    (q,) = take(1)
    bufs = take(len(sizes))
    state_in = {}
    for group in groups:
        m_in, l_in, acc_in = take(3)
        for at, i in enumerate(group):
            state_in[i] = (m_in, l_in, acc_in, at)
    (to_turn,) = take(1) if turn else (None,)
    if last:
        uv, wo_hbm = take(2)
        ho_out, *sent = take(1 + len({part for part, *_ in items}))
    else:
        acc, m_ref, l_ref = take(3)
        kv_out, direct = take(2) if gather else (None, None)
        (turned,) = take(1) if turn else (None,)
    kv, vt, cap, s_buf, p_buf, sems = take(6)
    if last:
        ho_t, *weights = refs
    keys = kv.shape[0]

    hist = 0
    if gather:
        hist, blk = kv_out.shape[0], own.shape[1]
        for k in range(hist // blk):
            fetch_block(listed, k, own, core, kv.at[pl.ds(k * blk, blk)], sems.at[0])
    weight_copies = start_weights(items, wo_hbm, weights, sems) if last else []

    at = 0
    for rows, is_new, limit_of in spans:
        limit = limit_of(cached[0])
        row = lax.broadcasted_iota(jnp.int32, (rows, tokens), 0)
        if is_new:
            limit = lax.broadcasted_iota(jnp.int32, (rows, tokens), 1) + 1 + limit
        cap[pl.ds(at, rows), :] = jnp.where(row < limit, pos_big, neg_big)
        at += rows
    at = hist
    for buf, rows in zip(bufs, sizes):
        kv[pl.ds(at, rows), :] = buf[...]
        at += rows
    if gather:
        fetched = kv.at[pl.ds(0, hist)]
        pltpu.make_async_copy(fetched, fetched, sems.at[0]).wait()
        for buf, size, start in ((kv, hist // 4, 0), (bufs[0], sizes[0] // 4, hist // 4)):
            rows = pl.ds(pl.multiple_of(quarter_of(3) * size, size), size)
            direct[pl.ds(start, size), :] = buf[rows, :]
        kv_out[...] = kv[0:hist, :]

    def scores(n):
        i = pairs[n]
        q_pair = jnp.concatenate([q[2 * i], q[2 * i + 1]], axis=1)
        s_buf[n % 2] = jnp.dot(kv[...], q_pair, preferred_element_type=jnp.float32)

    def fold(x):
        return x.reshape(CHUNK // 8, 8, x.shape[1])

    scores(0)
    vt[...] = kv[:, :lat].T
    for n, i in enumerate(pairs):
        if n + 1 < len(pairs):
            scores(n + 1)
        buf, weight = s_buf.at[n % 2], p_buf.at[n % 2]
        top = jnp.full((8, 2 * tokens), -jnp.inf, jnp.float32)
        for r in range(0, keys, CHUNK):
            limits = cap[r : r + CHUNK, :]
            x = jnp.minimum(buf[r : r + CHUNK, :], jnp.concatenate([limits, limits], axis=1))
            buf[r : r + CHUNK, :] = x
            top = jnp.maximum(top, jnp.max(fold(x), axis=0))
        m = jnp.max(top, axis=0, keepdims=True)
        if state_in:
            m_in, l_in, acc_in, at = state_in[i]
            m_old, l_old, acc_old = m_in[at], l_in[at], acc_in[at]
            m = jnp.maximum(m, m_old)
        scaled = m * exp2_scale
        total = jnp.zeros((8, 2 * tokens), jnp.float32)
        for r in range(0, keys, CHUNK):
            p = jnp.exp2(buf[r : r + CHUNK, :] * exp2_scale - scaled)
            total = total + jnp.sum(fold(p), axis=0)
            weight[r : r + CHUNK, :] = p.astype(jnp.bfloat16)
        l = jnp.sum(total, axis=0, keepdims=True)
        o = jnp.dot(vt[...], weight[...], preferred_element_type=jnp.float32)
        if state_in:
            factor = jnp.exp2(m_old * exp2_scale - scaled)
            l = l + l_old * factor
            o = o + acc_old * factor
        if not last:
            m_ref[n] = m
            l_ref[n] = l
            acc[n] = o
            continue
        latent = (o / l).astype(jnp.bfloat16)
        vh = uv.shape[1]
        for k in range(2):
            head = 2 * i + k
            out = jnp.dot(
                uv[head],
                latent[:, k * tokens : (k + 1) * tokens],
                preferred_element_type=jnp.float32,
            )
            ho_t[pl.ds(head * vh, vh), :] = out.astype(jnp.bfloat16)
    if turn:
        for head in range(turned.shape[0]):
            turned[head] = to_turn[head].T
    if last:
        ho_out[...] = ho_t[...].T
        project_items(items, ho_out, weight_copies, weights, sent)


def start_weights(items, wo_hbm, weights, sems):
    copies = []
    me = lax.axis_index("head")
    for n, (_, j, lo, width) in enumerate(items):
        cols = wo_hbm.shape[1] // lax.axis_size("head")
        start = pl.multiple_of((me ^ j) * cols + lo, LANES)
        copies.append(
            pltpu.make_async_copy(wo_hbm.at[:, pl.ds(start, width)], weights[n], sems.at[1 + n])
        )
        copies[-1].start()
    return copies


def project_items(items, head_out, copies, weights, outs):
    parts = sorted({part for part, *_ in items})
    filled = dict.fromkeys(parts, 0)
    for n, (part, _, _, _) in enumerate(items):
        copies[n].wait()
        value = jnp.dot(head_out[...], weights[n][...], preferred_element_type=jnp.float32)
        outs[parts.index(part)][filled[part]] = value.astype(jnp.bfloat16)
        filled[part] += 1


def item_shapes(items, tokens):
    sizes = {}
    for part, _, _, size in items:
        sizes[part] = (sizes.get(part, (0, size))[0] + 1, size)
    return [in_vmem((sizes[part][0], tokens, sizes[part][1])) for part in sorted(sizes)]


def attend(spans, cached, q_t, bufs, pairs, state, lat, gather=None, turn=None, last=None):
    heads, width, tokens = q_t.shape
    items = last[2] if last else ()
    keys = sum(rows for rows, *_ in spans)
    stat = (len(pairs), 1, 2 * tokens)
    flops = 4 * len(pairs) * tokens * keys * (width + lat)
    moved = 2 * keys * width
    inputs, specs = [pin(cached, pltpu.SMEM)], [SMEM_SPEC]
    if gather:
        listed, own, core, hist = gather
        inputs += [listed, pin(own, pltpu.HBM), pin(core, pltpu.VMEM)]
        specs += [SMEM_SPEC, HBM_SPEC, VMEM_SPEC]
    vmem = [q_t, *bufs]
    for _, arrays in state:
        vmem += arrays
    if turn is not None:
        vmem.append(turn)
    scratch = [
        pltpu.VMEM((keys, width), jnp.bfloat16),
        pltpu.VMEM((lat, keys), jnp.bfloat16),
        pltpu.VMEM((keys, tokens), jnp.float32),
        pltpu.VMEM((2, keys, 2 * tokens), jnp.float32),
        pltpu.VMEM((2, keys, 2 * tokens), jnp.bfloat16),
        pltpu.SemaphoreType.DMA((1 + len(items),)),
    ]
    if last:
        up, proj, _ = last
        vmem.append(up)
        out_shape = [in_vmem((tokens, heads * up.shape[1])), *item_shapes(items, tokens)]
        scratch.append(pltpu.VMEM((heads * up.shape[1], tokens), jnp.bfloat16))
        for _, _, _, size in items:
            scratch.append(pltpu.VMEM((proj.shape[0], size), jnp.bfloat16))
            flops += 2 * tokens * proj.shape[0] * size
            moved += 2 * proj.shape[0] * size
    else:
        out_shape = [
            in_vmem((len(pairs), lat, 2 * tokens), jnp.float32),
            in_vmem(stat, jnp.float32),
            in_vmem(stat, jnp.float32),
        ]
        if gather:
            out_shape += [in_vmem((hist, width)), in_vmem(((hist + bufs[0].shape[0]) // 4, width))]
        if turn is not None:
            out_shape.append(in_vmem((turn.shape[0], turn.shape[2], turn.shape[1])))
    inputs += [pin(value, pltpu.VMEM) for value in vmem]
    specs += [VMEM_SPEC] * len(vmem)
    if last:
        inputs.append(pin(proj, pltpu.HBM))
        specs.append(HBM_SPEC)
    groups = tuple(group for group, _ in state)
    sizes = tuple(buf.shape[0] for buf in bufs)
    cfg = (
        tuple(spans), sizes, pairs, groups, bool(gather), turn is not None, bool(last), tokens, lat,
        items,
    )
    outs = pl.pallas_call(
        functools.partial(attend_kernel, cfg),
        out_shape=out_shape,
        in_specs=specs,
        out_specs=[VMEM_SPEC] * len(out_shape),
        scratch_shapes=scratch,
        compiler_params=pltpu.CompilerParams(vmem_limit_bytes=24 << 20),
        cost_estimate=pl.CostEstimate(
            flops=flops, bytes_accessed=moved, transcendentals=2 * len(pairs) * tokens * keys
        ),
        name="attend_last" if last else "attend_gather" if gather else "attend",
    )(*inputs)
    return outs if last else ((pairs, (outs[1], outs[2], outs[0])), *outs[3:])


def project_kernel(items, head_out, wo_hbm, *refs):
    parts = len({part for part, *_ in items})
    outs, (sems, *weights) = refs[:parts], refs[parts:]
    copies = start_weights(items, wo_hbm, weights, sems)
    project_items(items, head_out, copies, weights, outs)


def project(head_out, proj, items, name):
    tokens, depth = head_out.shape
    out_shape = item_shapes(items, tokens)
    columns = sum(size for _, _, _, size in items)
    return pl.pallas_call(
        functools.partial(project_kernel, items),
        out_shape=out_shape,
        in_specs=[VMEM_SPEC, HBM_SPEC],
        out_specs=[VMEM_SPEC] * len(out_shape),
        scratch_shapes=[pltpu.SemaphoreType.DMA((1 + len(items),))]
        + [pltpu.VMEM((depth, size), jnp.bfloat16) for _, _, _, size in items],
        compiler_params=pltpu.CompilerParams(vmem_limit_bytes=16 << 20),
        cost_estimate=pl.CostEstimate(
            flops=2 * tokens * depth * columns, bytes_accessed=2 * depth * columns, transcendentals=0
        ),
        name=name,
    )(pin(head_out, pltpu.VMEM), pin(proj, pltpu.HBM))


def flip_bit(value, axis, bit):
    size = lax.axis_size(axis)
    return lax.ppermute(value, axis, [(i, i ^ (1 << bit)) for i in range(size)])


def from_ahead(value, steps):
    size = lax.axis_size("ctx")
    return lax.ppermute(value, "ctx", [((i + steps) % size, i) for i in range(size)])


def add_halves(a, b):
    return (a.astype(jnp.float32) + b.astype(jnp.float32)).astype(jnp.bfloat16)


def sum_to_owner(keep, send, order):
    for stage, bit in enumerate(order):
        got = flip_bit(send, "head", bit)
        if stage + 1 == len(order):
            return keep[0].astype(jnp.float32) + got[0].astype(jnp.float32)
        half = keep.shape[0] // 2
        send = add_halves(keep[half:], got[half:])
        keep = add_halves(keep[:half], got[:half])


def tie(*values):
    return lax.optimization_barrier(values)


def body(queries, new_latent, cache_pool, block_list, cached_lengths, w_uv, w_o):
    n_ctx = lax.axis_size("ctx")
    n_head = lax.axis_size("head")
    own = cache_pool[0]
    slots, blk, width = own.shape
    tokens = queries.shape[1]
    lat = w_uv.shape[1]
    blocks = block_list.shape[2]
    hist = blocks * blk
    part = hist // 4
    new_part = tokens // 4
    new_own = new_latent[0]
    proj = w_o.reshape(w_o.shape[0] * w_o.shape[1], w_o.shape[2])
    q_t = jnp.transpose(queries[0], (1, 2, 0))
    cols = proj.shape[1] // n_head
    pairs = tuple(range(q_t.shape[0] // 2))
    pairs_a, pairs_b = pairs[: (len(pairs) + 1) // 2], pairs[(len(pairs) + 1) // 2 :]

    def source_of(step):
        return lax.rem(lax.axis_index("ctx") + step, n_ctx)

    def piece_spans(step, flip):
        def history(cached):
            return cached - source_of(step) * hist - part * quarter_of(flip)

        def new(cached):
            ahead = (lax.axis_index("ctx") - source_of(step)) * tokens
            return ahead - new_part * quarter_of(flip)

        return [(part, False, history), (new_part, True, new)]

    own_spans = [
        (hist, False, lambda cached: cached - lax.axis_index("ctx") * hist),
        (tokens, True, lambda cached: 0),
    ]

    core = flip_bit(own, "pool", 0)
    listed = block_list[0, 0] - slots * lax.axis_index("pool")
    piece = pick_quarter(listed, own, core, new_own, blocks // 4)
    by_x = from_ahead(piece, 1)
    begun, kv_own, direct = attend(
        own_spans, cached_lengths, q_t, [new_own], pairs_a, [], lat, gather=(listed, own, core, hist)
    )
    by_x, direct, kv_own = tie(by_x, direct, kv_own)
    state = [begun]
    arrivals = []
    for step in range(1, n_ctx):
        if step > 1:
            by_x = from_ahead(piece, step)
        by_y = flip_bit(by_x, "head", 0)
        by_z = flip_bit(by_x, "head", 1)
        arrivals.append((by_x, by_y, by_z, from_ahead(direct, step)))
    if pairs_b:
        state += attend(own_spans, cached_lengths, q_t, [kv_own, new_own], pairs_b, [], lat)

    bits = n_head.bit_length() - 1
    half = n_head // 2
    if cols % LANES == 0 and n_head == 8:
        wide = -(-cols // (2 * LANES)) * LANES
        orders = (tuple(range(bits)), (1, 0) + tuple(range(2, bits)))
        spans = ((0, wide), (wide, cols - wide))
        ranked = [
            [(part, j, *spans[part]) for j in slot_order(order)] for part, order in enumerate(orders)
        ]
        sends = tuple(ranked[0][half:] + ranked[1][half:])
        keeps = tuple(ranked[0][:half] + ranked[1][:half])
    else:
        orders, sends = (), ()

    up = None
    for step in range(1, n_ctx):
        by_x, *others = arrivals[step - 1]
        spans = piece_spans(step, 0)
        begun, *turned = attend(
            spans, cached_lengths, q_t, [by_x], pairs, state, lat, turn=w_uv if up is None else None
        )
        up = turned[0] if turned else up
        state = [begun]
        spans = piece_spans(step, 1) + piece_spans(step, 2) + piece_spans(step, 3)
        if step + 1 < n_ctx:
            state = attend(spans, cached_lengths, q_t, others, pairs, state, lat)
    head_out, *sent = attend(
        spans, cached_lengths, q_t, others, pairs, state, lat, last=(up, proj, sends)
    )
    if orders:
        kept = project(head_out, proj, keeps, "project_kept")
        done = [sum_to_owner(k, s, order) for k, s, order in zip(kept, sent, orders)]
        return jnp.concatenate(done, axis=1).astype(jnp.bfloat16)[None]
    partial_out = jnp.dot(head_out, proj, preferred_element_type=jnp.float32)
    blocks = jnp.transpose(partial_out.reshape(tokens, n_head, cols), (1, 0, 2)).astype(jnp.bfloat16)
    order = tuple(range(bits))
    mine = lax.axis_index("head") ^ jnp.array(slot_order(order), jnp.int32)
    blocks = jnp.take(blocks, mine, axis=0)
    return sum_to_owner(blocks[:half], blocks[half:], order).astype(jnp.bfloat16)[None]


def solution(mesh):
    in_specs = (
        P("pool", "ctx", "head", None),
        P("pool", "ctx", None),
        P("ctx", "pool", None, None),
        P("pool", "ctx", None),
        P("pool"),
        P("head", None, None),
        P("head", None, None),
    )
    out_specs = P("pool", "ctx", "head")
    return jax.shard_map(body, mesh=mesh, in_specs=in_specs, out_specs=out_specs, check_vma=False)
```

```python
import functools

import jax
import jax.numpy as jnp
from jax import lax
from jax.experimental import pallas as pl
from jax.experimental.pallas import tpu as pltpu
from jax.sharding import PartitionSpec as P

score_scale = 192.0 ** (-0.5)
log2_e = 1.4426950408889634
exp2_scale = score_scale * log2_e
neg_big = -1e30
pos_big = 3e38
LANES = 128
CHUNK = 96
ANY_SPEC = pl.BlockSpec(memory_space=pl.ANY)
HBM_SPEC = pl.BlockSpec(memory_space=pltpu.HBM)
VMEM_SPEC = pl.BlockSpec(memory_space=pltpu.VMEM)
SMEM_SPEC = pl.BlockSpec(memory_space=pltpu.SMEM)


def slot_order(order):
    bits = len(order)
    return [
        sum(((rank >> (bits - 1 - i)) & 1) << order[i] for i in range(bits))
        for rank in range(1 << bits)
    ]


def in_vmem(shape, dtype=jnp.bfloat16):
    return pltpu.VMEM(shape, dtype)


def pin(value, space):
    return pltpu.with_memory_space_constraint(value, space)


def fetch_block(listed, k, own, core, target, sem):
    slots = own.shape[0]
    slot = listed[k]
    place = slot & (slots - 1)
    here = (slot >= 0) & (slot < slots)

    @pl.when(here)
    def _():
        pltpu.make_async_copy(own.at[place], target, sem).start()

    @pl.when(jnp.logical_not(here))
    def _():
        pltpu.make_async_copy(core.at[place], target, sem).start()


def quarter_of(flip):
    return (lax.axis_index("head") & 3) ^ flip


def pick_kernel(quarter, listed, own, core, new, piece, sem):
    blk = own.shape[1]
    part = new.shape[0] // 4
    for j in range(quarter):
        target = piece.at[pl.ds(j * blk, blk)]
        fetch_block(listed, quarter * quarter_of(0) + j, own, core, target, sem.at[0])
    rows = pl.ds(pl.multiple_of(quarter_of(0) * part, part), part)
    piece[pl.ds(quarter * blk, part), :] = new[rows, :]
    fetched = piece.at[pl.ds(0, quarter * blk)]
    pltpu.make_async_copy(fetched, fetched, sem.at[0]).wait()


def pick_quarter(listed, own, core, new, quarter):
    _, blk, width = own.shape
    return pl.pallas_call(
        functools.partial(pick_kernel, quarter),
        out_shape=in_vmem((quarter * blk + new.shape[0] // 4, width)),
        in_specs=[SMEM_SPEC, HBM_SPEC, VMEM_SPEC, VMEM_SPEC],
        out_specs=VMEM_SPEC,
        scratch_shapes=[pltpu.SemaphoreType.DMA((1,))],
        compiler_params=pltpu.CompilerParams(vmem_limit_bytes=4 << 20),
        cost_estimate=pl.CostEstimate(
            flops=0, bytes_accessed=4 * quarter * blk * width, transcendentals=0
        ),
        name="pick_quarter",
    )(listed, pin(own, pltpu.HBM), pin(core, pltpu.VMEM), pin(new, pltpu.VMEM))


def attend_kernel(cfg, *refs):
    spans, sizes, pairs, groups, gather, turn, last, tokens, lat, items = cfg
    refs = list(refs)
    take = lambda n: [refs.pop(0) for _ in range(n)]
    (cached,) = take(1)
    listed, own, core = take(3) if gather else (None, None, None)
    (q,) = take(1)
    bufs = take(len(sizes))
    state_in = {}
    for group in groups:
        m_in, l_in, acc_in = take(3)
        for at, i in enumerate(group):
            state_in[i] = (m_in, l_in, acc_in, at)
    (to_turn,) = take(1) if turn else (None,)
    if last:
        uv, wo_hbm = take(2)
        ho_out, *sent = take(1 + len({part for part, *_ in items}))
    else:
        acc, m_ref, l_ref = take(3)
        kv_out, direct = take(2) if gather else (None, None)
        (turned,) = take(1) if turn else (None,)
    kv, vt, cap, s_buf, p_buf, sems = take(6)
    if last:
        ho_t, *weights = refs
    keys = kv.shape[0]

    hist = 0
    if gather:
        hist, blk = kv_out.shape[0], own.shape[1]
        for k in range(hist // blk):
            fetch_block(listed, k, own, core, kv.at[pl.ds(k * blk, blk)], sems.at[0])
    weight_copies = start_weights(items, wo_hbm, weights, sems) if last else []

    at = 0
    for rows, is_new, limit_of in spans:
        limit = limit_of(cached[0])
        row = lax.broadcasted_iota(jnp.int32, (rows, tokens), 0)
        if is_new:
            limit = lax.broadcasted_iota(jnp.int32, (rows, tokens), 1) + 1 + limit
        cap[pl.ds(at, rows), :] = jnp.where(row < limit, pos_big, neg_big)
        at += rows
    at = hist
    for buf, rows in zip(bufs, sizes):
        kv[pl.ds(at, rows), :] = buf[...]
        at += rows
    if gather:
        fetched = kv.at[pl.ds(0, hist)]
        pltpu.make_async_copy(fetched, fetched, sems.at[0]).wait()
        for buf, size, start in ((kv, hist // 4, 0), (bufs[0], sizes[0] // 4, hist // 4)):
            rows = pl.ds(pl.multiple_of(quarter_of(3) * size, size), size)
            direct[pl.ds(start, size), :] = buf[rows, :]
        kv_out[...] = kv[0:hist, :]

    def scores(n):
        i = pairs[n]
        q_pair = jnp.concatenate([q[2 * i], q[2 * i + 1]], axis=1)
        s_buf[n % 2] = jnp.dot(kv[...], q_pair, preferred_element_type=jnp.float32)

    def fold(x):
        return x.reshape(CHUNK // 8, 8, x.shape[1])

    scores(0)
    vt[...] = kv[:, :lat].T
    for n, i in enumerate(pairs):
        if n + 1 < len(pairs):
            scores(n + 1)
        buf, weight = s_buf.at[n % 2], p_buf.at[n % 2]
        top = jnp.full((8, 2 * tokens), -jnp.inf, jnp.float32)
        for r in range(0, keys, CHUNK):
            limits = cap[r : r + CHUNK, :]
            x = jnp.minimum(buf[r : r + CHUNK, :], jnp.concatenate([limits, limits], axis=1))
            buf[r : r + CHUNK, :] = x
            top = jnp.maximum(top, jnp.max(fold(x), axis=0))
        m = jnp.max(top, axis=0, keepdims=True)
        if state_in:
            m_in, l_in, acc_in, at = state_in[i]
            m_old, l_old, acc_old = m_in[at], l_in[at], acc_in[at]
            m = jnp.maximum(m, m_old)
        scaled = m * exp2_scale
        total = jnp.zeros((8, 2 * tokens), jnp.float32)
        for r in range(0, keys, CHUNK):
            p = jnp.exp2(buf[r : r + CHUNK, :] * exp2_scale - scaled)
            total = total + jnp.sum(fold(p), axis=0)
            weight[r : r + CHUNK, :] = p.astype(jnp.bfloat16)
        l = jnp.sum(total, axis=0, keepdims=True)
        o = jnp.dot(vt[...], weight[...], preferred_element_type=jnp.float32)
        if state_in:
            factor = jnp.exp2(m_old * exp2_scale - scaled)
            l = l + l_old * factor
            o = o + acc_old * factor
        if not last:
            m_ref[n] = m
            l_ref[n] = l
            acc[n] = o
            continue
        latent = (o / l).astype(jnp.bfloat16)
        vh = uv.shape[1]
        for k in range(2):
            head = 2 * i + k
            out = jnp.dot(
                uv[head],
                latent[:, k * tokens : (k + 1) * tokens],
                preferred_element_type=jnp.float32,
            )
            ho_t[pl.ds(head * vh, vh), :] = out.astype(jnp.bfloat16)
    if turn:
        for head in range(turned.shape[0]):
            turned[head] = to_turn[head].T
    if last:
        ho_out[...] = ho_t[...].T
        project_items(items, ho_out, weight_copies, weights, sent)


def start_weights(items, wo_hbm, weights, sems):
    copies, filled = [], {}
    parts = sorted({part for part, *_ in items})
    me = lax.axis_index("head")
    cols = wo_hbm.shape[1] // lax.axis_size("head")
    for n, (part, j, lo, width) in enumerate(items):
        at = filled.get(part, 0)
        filled[part] = at + width
        copies.append(
            pltpu.make_async_copy(
                wo_hbm.at[:, pl.ds(pl.multiple_of((me ^ j) * cols + lo, LANES), width)],
                weights[parts.index(part)].at[:, pl.ds(at, width)],
                sems.at[1 + n],
            )
        )
        copies[-1].start()
    return copies


def project_items(items, head_out, copies, weights, outs):
    parts = sorted({part for part, *_ in items})
    for n, part in enumerate(parts):
        widths = [width for other, _, _, width in items if other == part]
        for copy, (other, *_) in zip(copies, items):
            if other == part:
                copy.wait()
        value = jnp.dot(head_out[...], weights[n][...], preferred_element_type=jnp.float32)
        for at, width in enumerate(widths):
            outs[n][at] = value[:, at * width : (at + 1) * width].astype(jnp.bfloat16)


def weight_shapes(items, depth):
    sizes = {}
    for part, _, _, width in items:
        sizes[part] = sizes.get(part, 0) + width
    return [pltpu.VMEM((depth, sizes[part]), jnp.bfloat16) for part in sorted(sizes)]


def item_shapes(items, tokens):
    sizes = {}
    for part, _, _, size in items:
        sizes[part] = (sizes.get(part, (0, size))[0] + 1, size)
    return [in_vmem((sizes[part][0], tokens, sizes[part][1])) for part in sorted(sizes)]


def attend(spans, cached, q_t, bufs, pairs, state, lat, gather=None, turn=None, last=None):
    heads, width, tokens = q_t.shape
    items = last[2] if last else ()
    keys = sum(rows for rows, *_ in spans)
    stat = (len(pairs), 1, 2 * tokens)
    flops = 4 * len(pairs) * tokens * keys * (width + lat)
    moved = 2 * keys * width
    inputs, specs = [pin(cached, pltpu.SMEM)], [SMEM_SPEC]
    if gather:
        listed, own, core, hist = gather
        inputs += [listed, pin(own, pltpu.HBM), pin(core, pltpu.VMEM)]
        specs += [SMEM_SPEC, HBM_SPEC, VMEM_SPEC]
    vmem = [q_t, *bufs]
    for _, arrays in state:
        vmem += arrays
    if turn is not None:
        vmem.append(turn)
    scratch = [
        pltpu.VMEM((keys, width), jnp.bfloat16),
        pltpu.VMEM((lat, keys), jnp.bfloat16),
        pltpu.VMEM((keys, tokens), jnp.float32),
        pltpu.VMEM((2, keys, 2 * tokens), jnp.float32),
        pltpu.VMEM((2, keys, 2 * tokens), jnp.bfloat16),
        pltpu.SemaphoreType.DMA((1 + len(items),)),
    ]
    if last:
        up, proj, _ = last
        vmem.append(up)
        out_shape = [in_vmem((tokens, heads * up.shape[1])), *item_shapes(items, tokens)]
        scratch.append(pltpu.VMEM((heads * up.shape[1], tokens), jnp.bfloat16))
        scratch += weight_shapes(items, proj.shape[0])
        columns = sum(size for _, _, _, size in items)
        flops += 2 * tokens * proj.shape[0] * columns
        moved += 2 * proj.shape[0] * columns
    else:
        out_shape = [
            in_vmem((len(pairs), lat, 2 * tokens), jnp.float32),
            in_vmem(stat, jnp.float32),
            in_vmem(stat, jnp.float32),
        ]
        if gather:
            out_shape += [in_vmem((hist, width)), in_vmem(((hist + bufs[0].shape[0]) // 4, width))]
        if turn is not None:
            out_shape.append(in_vmem((turn.shape[0], turn.shape[2], turn.shape[1])))
    inputs += [pin(value, pltpu.VMEM) for value in vmem]
    specs += [VMEM_SPEC] * len(vmem)
    if last:
        inputs.append(pin(proj, pltpu.HBM))
        specs.append(HBM_SPEC)
    groups = tuple(group for group, _ in state)
    sizes = tuple(buf.shape[0] for buf in bufs)
    cfg = (
        tuple(spans), sizes, pairs, groups, bool(gather), turn is not None, bool(last), tokens, lat,
        items,
    )
    outs = pl.pallas_call(
        functools.partial(attend_kernel, cfg),
        out_shape=out_shape,
        in_specs=specs,
        out_specs=[VMEM_SPEC] * len(out_shape),
        scratch_shapes=scratch,
        compiler_params=pltpu.CompilerParams(vmem_limit_bytes=24 << 20),
        cost_estimate=pl.CostEstimate(
            flops=flops, bytes_accessed=moved, transcendentals=2 * len(pairs) * tokens * keys
        ),
        name="attend_last" if last else "attend_gather" if gather else "attend",
    )(*inputs)
    return outs if last else ((pairs, (outs[1], outs[2], outs[0])), *outs[3:])


def project_kernel(items, head_out, wo_hbm, *refs):
    parts = len({part for part, *_ in items})
    outs, (sems, *weights) = refs[:parts], refs[parts:]
    copies = start_weights(items, wo_hbm, weights, sems)
    project_items(items, head_out, copies, weights, outs)


def project(head_out, proj, items, name):
    tokens, depth = head_out.shape
    out_shape = item_shapes(items, tokens)
    columns = sum(size for _, _, _, size in items)
    return pl.pallas_call(
        functools.partial(project_kernel, items),
        out_shape=out_shape,
        in_specs=[VMEM_SPEC, HBM_SPEC],
        out_specs=[VMEM_SPEC] * len(out_shape),
        scratch_shapes=[pltpu.SemaphoreType.DMA((1 + len(items),))]
        + weight_shapes(items, depth),
        compiler_params=pltpu.CompilerParams(vmem_limit_bytes=16 << 20),
        cost_estimate=pl.CostEstimate(
            flops=2 * tokens * depth * columns, bytes_accessed=2 * depth * columns, transcendentals=0
        ),
        name=name,
    )(pin(head_out, pltpu.VMEM), pin(proj, pltpu.HBM))


def flip_bit(value, axis, bit):
    size = lax.axis_size(axis)
    return lax.ppermute(value, axis, [(i, i ^ (1 << bit)) for i in range(size)])


def from_ahead(value, steps):
    size = lax.axis_size("ctx")
    return lax.ppermute(value, "ctx", [((i + steps) % size, i) for i in range(size)])


def add_halves(a, b):
    return (a.astype(jnp.float32) + b.astype(jnp.float32)).astype(jnp.bfloat16)


def sum_to_owner(keep, send, order):
    for stage, bit in enumerate(order):
        got = flip_bit(send, "head", bit)
        if stage + 1 == len(order):
            return keep[0].astype(jnp.float32) + got[0].astype(jnp.float32)
        half = keep.shape[0] // 2
        send = add_halves(keep[half:], got[half:])
        keep = add_halves(keep[:half], got[:half])


def tie(*values):
    return lax.optimization_barrier(values)


def body(queries, new_latent, cache_pool, block_list, cached_lengths, w_uv, w_o):
    n_ctx = lax.axis_size("ctx")
    n_head = lax.axis_size("head")
    own = cache_pool[0]
    slots, blk, width = own.shape
    tokens = queries.shape[1]
    lat = w_uv.shape[1]
    blocks = block_list.shape[2]
    hist = blocks * blk
    part = hist // 4
    new_part = tokens // 4
    new_own = new_latent[0]
    proj = w_o.reshape(w_o.shape[0] * w_o.shape[1], w_o.shape[2])
    q_t = jnp.transpose(queries[0], (1, 2, 0))
    cols = proj.shape[1] // n_head
    pairs = tuple(range(q_t.shape[0] // 2))
    pairs_a, pairs_b = pairs[: (len(pairs) + 1) // 2], pairs[(len(pairs) + 1) // 2 :]

    def source_of(step):
        return lax.rem(lax.axis_index("ctx") + step, n_ctx)

    def piece_spans(step, flip):
        def history(cached):
            return cached - source_of(step) * hist - part * quarter_of(flip)

        def new(cached):
            ahead = (lax.axis_index("ctx") - source_of(step)) * tokens
            return ahead - new_part * quarter_of(flip)

        return [(part, False, history), (new_part, True, new)]

    own_spans = [
        (hist, False, lambda cached: cached - lax.axis_index("ctx") * hist),
        (tokens, True, lambda cached: 0),
    ]

    core = flip_bit(own, "pool", 0)
    listed = block_list[0, 0] - slots * lax.axis_index("pool")
    piece = pick_quarter(listed, own, core, new_own, blocks // 4)
    by_x = from_ahead(piece, 1)
    begun, kv_own, direct = attend(
        own_spans, cached_lengths, q_t, [new_own], pairs_a, [], lat, gather=(listed, own, core, hist)
    )
    by_x, direct, kv_own = tie(by_x, direct, kv_own)
    state = [begun]
    arrivals = []
    for step in range(1, n_ctx):
        if step > 1:
            by_x = from_ahead(piece, step)
        by_y = flip_bit(by_x, "head", 0)
        by_z = flip_bit(by_x, "head", 1)
        arrivals.append((by_x, by_y, by_z, from_ahead(direct, step)))
    if pairs_b:
        state += attend(own_spans, cached_lengths, q_t, [kv_own, new_own], pairs_b, [], lat)

    bits = n_head.bit_length() - 1
    half = n_head // 2
    if cols % LANES == 0 and n_head == 8:
        narrow = cols // (2 * LANES) * LANES
        orders = (tuple(range(bits)), (1, 0) + tuple(range(2, bits)))
        spans = ((0, narrow), (narrow, cols - narrow))
        ranked = [
            [(part, j, *spans[part]) for j in slot_order(order)] for part, order in enumerate(orders)
        ]
        sends = tuple(item for ranks in ranked for item in ranks[half:])
        keeps = tuple(item for ranks in ranked for item in ranks[:half])
    else:
        orders, sends = (), ()

    up = None
    for step in range(1, n_ctx):
        by_x, *others = arrivals[step - 1]
        spans = piece_spans(step, 0)
        begun, *turned = attend(
            spans, cached_lengths, q_t, [by_x], pairs, state, lat, turn=w_uv if up is None else None
        )
        up = turned[0] if turned else up
        state = [begun]
        spans = piece_spans(step, 1) + piece_spans(step, 2) + piece_spans(step, 3)
        if step + 1 < n_ctx:
            state = attend(spans, cached_lengths, q_t, others, pairs, state, lat)
    head_out, *sent = attend(
        spans, cached_lengths, q_t, others, pairs, state, lat, last=(up, proj, sends)
    )
    if orders:
        kept = project(head_out, proj, keeps, "project_kept")
        done = [sum_to_owner(k, s, order) for k, s, order in zip(kept, sent, orders)]
        return jnp.concatenate(done, axis=1).astype(jnp.bfloat16)[None]
    partial_out = jnp.dot(head_out, proj, preferred_element_type=jnp.float32)
    blocks = jnp.transpose(partial_out.reshape(tokens, n_head, cols), (1, 0, 2)).astype(jnp.bfloat16)
    order = tuple(range(bits))
    mine = lax.axis_index("head") ^ jnp.array(slot_order(order), jnp.int32)
    blocks = jnp.take(blocks, mine, axis=0)
    return sum_to_owner(blocks[:half], blocks[half:], order).astype(jnp.bfloat16)[None]


def solution(mesh):
    in_specs = (
        P("pool", "ctx", "head", None),
        P("pool", "ctx", None),
        P("ctx", "pool", None, None),
        P("pool", "ctx", None),
        P("pool"),
        P("head", None, None),
        P("head", None, None),
    )
    out_specs = P("pool", "ctx", "head")
    return jax.shard_map(body, mesh=mesh, in_specs=in_specs, out_specs=out_specs, check_vma=False)
```

```python
import functools

import jax
import jax.numpy as jnp
from jax import lax
from jax.experimental import pallas as pl
from jax.experimental.pallas import tpu as pltpu
from jax.sharding import PartitionSpec as P

score_scale = 192.0 ** (-0.5)
log2_e = 1.4426950408889634
exp2_scale = score_scale * log2_e
neg_big = -1e30
pos_big = 3e38
LANES = 128
CHUNK = 96
ANY_SPEC = pl.BlockSpec(memory_space=pl.ANY)
HBM_SPEC = pl.BlockSpec(memory_space=pltpu.HBM)
VMEM_SPEC = pl.BlockSpec(memory_space=pltpu.VMEM)
SMEM_SPEC = pl.BlockSpec(memory_space=pltpu.SMEM)


def slot_order(order):
    bits = len(order)
    return [
        sum(((rank >> (bits - 1 - i)) & 1) << order[i] for i in range(bits))
        for rank in range(1 << bits)
    ]


def in_vmem(shape, dtype=jnp.bfloat16):
    return pltpu.VMEM(shape, dtype)


def pin(value, space):
    return pltpu.with_memory_space_constraint(value, space)


def block_place(listed, k, slots):
    slot = listed[k]
    return slot & (slots - 1), (slot >= 0) & (slot < slots)


def fetch_blocks(listed, ks, own, core, rows, sem):
    slots, blk, _ = own.shape
    targets = [rows.at[pl.ds(n * blk, blk)] for n in range(len(ks))]
    for k, target in zip(ks, targets):
        place, here = block_place(listed, k, slots)

        @pl.when(here)
        def _(place=place, target=target):
            pltpu.make_async_copy(own.at[place], target, sem).start()

    for k, target in zip(ks, targets):
        place, here = block_place(listed, k, slots)

        @pl.when(jnp.logical_not(here))
        def _(place=place, target=target):
            target[...] = core[place]

    def finish():
        for k, target in zip(ks, targets):
            place, here = block_place(listed, k, slots)

            @pl.when(here)
            def _(place=place, target=target):
                pltpu.make_async_copy(own.at[place], target, sem).wait()

    return finish


def quarter_of(flip):
    return (lax.axis_index("head") & 3) ^ flip


def packed_shape(rows, width):
    return (rows * width // LANES, LANES)


def pack(rows, packed):
    count, width = rows.shape
    whole = width // LANES
    for i in range(whole):
        packed[i * count : (i + 1) * count, :] = rows[:, i * LANES : (i + 1) * LANES]
    half = count // 2
    rest = whole * LANES
    packed[whole * count :, :] = jnp.concatenate([rows[0:half, rest:], rows[half:, rest:]], axis=1)


def unpack(packed, rows, at, count):
    width = rows.shape[1]
    whole = width // LANES
    for i in range(whole):
        rows[at : at + count, i * LANES : (i + 1) * LANES] = packed[i * count : (i + 1) * count, :]
    half = count // 2
    rest = whole * LANES
    rows[at : at + half, rest:] = packed[whole * count :, : width - rest]
    rows[at + half : at + count, rest:] = packed[whole * count :, width - rest :]


def pick_kernel(quarter, listed, own, core, new, piece, rows, sem):
    blk = own.shape[1]
    part = new.shape[0] // 4
    ks = [quarter * quarter_of(0) + j for j in range(quarter)]
    finish = fetch_blocks(listed, ks, own, core, rows, sem.at[0])
    mine = pl.ds(pl.multiple_of(quarter_of(0) * part, part), part)
    rows[pl.ds(quarter * blk, part), :] = new[mine, :]
    finish()
    pack(rows, piece)


def pick_quarter(listed, own, core, new, quarter):
    _, blk, width = own.shape
    rows = quarter * blk + new.shape[0] // 4
    return pl.pallas_call(
        functools.partial(pick_kernel, quarter),
        out_shape=in_vmem(packed_shape(rows, width)),
        in_specs=[SMEM_SPEC, HBM_SPEC, VMEM_SPEC, VMEM_SPEC],
        out_specs=VMEM_SPEC,
        scratch_shapes=[pltpu.VMEM((rows, width), jnp.bfloat16), pltpu.SemaphoreType.DMA((1,))],
        compiler_params=pltpu.CompilerParams(vmem_limit_bytes=8 << 20),
        cost_estimate=pl.CostEstimate(
            flops=0, bytes_accessed=4 * quarter * blk * width, transcendentals=0
        ),
        name="pick_quarter",
    )(listed, pin(own, pltpu.HBM), pin(core, pltpu.VMEM), pin(new, pltpu.VMEM))


def attend_kernel(cfg, *refs):
    spans, sizes, pairs, groups, gather, turn, last, tokens, lat, items = cfg
    refs = list(refs)
    take = lambda n: [refs.pop(0) for _ in range(n)]
    (cached,) = take(1)
    listed, own, core = take(3) if gather else (None, None, None)
    (q,) = take(1)
    bufs = take(len(sizes))
    state_in = {}
    for group in groups:
        m_in, l_in, acc_in = take(3)
        for at, i in enumerate(group):
            state_in[i] = (m_in, l_in, acc_in, at)
    (to_turn,) = take(1) if turn else (None,)
    if last:
        uv, wo_hbm = take(2)
        ho_out, *sent = take(1 + len({part for part, *_ in items}))
    else:
        acc, m_ref, l_ref = take(3)
        kv_out, direct = take(2) if gather else (None, None)
        (turned,) = take(1) if turn else (None,)
    kv, vt, cap, s_buf, p_buf, sems = take(6)
    (far_rows,) = take(1) if gather else (None,)
    if last:
        ho_t, *weights = refs
    keys = kv.shape[0]

    hist = 0
    if gather:
        hist, blk = kv_out.shape[0], own.shape[1]
        finish = fetch_blocks(listed, range(hist // blk), own, core, kv, sems.at[0])
    weight_copies = start_weights(items, wo_hbm, weights, sems) if last else []

    at = 0
    for rows, is_new, limit_of in spans:
        limit = limit_of(cached[0])
        row = lax.broadcasted_iota(jnp.int32, (rows, tokens), 0)
        if is_new:
            limit = lax.broadcasted_iota(jnp.int32, (rows, tokens), 1) + 1 + limit
        cap[pl.ds(at, rows), :] = jnp.where(row < limit, pos_big, neg_big)
        at += rows
    at = hist
    for buf, (rows, packed) in zip(bufs, sizes):
        if packed:
            unpack(buf, kv, at, rows)
        else:
            kv[pl.ds(at, rows), :] = buf[...]
        at += rows
    if gather:
        finish()
        for buf, size, start in ((kv, hist // 4, 0), (bufs[0], sizes[0][0] // 4, hist // 4)):
            rows = pl.ds(pl.multiple_of(quarter_of(3) * size, size), size)
            far_rows[pl.ds(start, size), :] = buf[rows, :]
        pack(far_rows, direct)
        kv_out[...] = kv[0:hist, :]

    def scores(n):
        i = pairs[n]
        q_pair = jnp.concatenate([q[2 * i], q[2 * i + 1]], axis=1)
        s_buf[n % 2] = jnp.dot(kv[...], q_pair, preferred_element_type=jnp.float32)

    def fold(x):
        return x.reshape(CHUNK // 8, 8, x.shape[1])

    scores(0)
    vt[...] = kv[:, :lat].T
    for n, i in enumerate(pairs):
        if n + 1 < len(pairs):
            scores(n + 1)
        buf, weight = s_buf.at[n % 2], p_buf.at[n % 2]
        top = jnp.full((8, 2 * tokens), -jnp.inf, jnp.float32)
        for r in range(0, keys, CHUNK):
            limits = cap[r : r + CHUNK, :]
            x = jnp.minimum(buf[r : r + CHUNK, :], jnp.concatenate([limits, limits], axis=1))
            buf[r : r + CHUNK, :] = x
            top = jnp.maximum(top, jnp.max(fold(x), axis=0))
        m = jnp.max(top, axis=0, keepdims=True)
        if state_in:
            m_in, l_in, acc_in, at = state_in[i]
            m_old, l_old, acc_old = m_in[at], l_in[at], acc_in[at]
            m = jnp.maximum(m, m_old)
        scaled = m * exp2_scale
        total = jnp.zeros((8, 2 * tokens), jnp.float32)
        for r in range(0, keys, CHUNK):
            p = jnp.exp2(buf[r : r + CHUNK, :] * exp2_scale - scaled)
            total = total + jnp.sum(fold(p), axis=0)
            weight[r : r + CHUNK, :] = p.astype(jnp.bfloat16)
        l = jnp.sum(total, axis=0, keepdims=True)
        o = jnp.dot(vt[...], weight[...], preferred_element_type=jnp.float32)
        if state_in:
            factor = jnp.exp2(m_old * exp2_scale - scaled)
            l = l + l_old * factor
            o = o + acc_old * factor
        if not last:
            m_ref[n] = m
            l_ref[n] = l
            acc[n] = o
            continue
        latent = (o / l).astype(jnp.bfloat16)
        vh = uv.shape[1]
        for k in range(2):
            head = 2 * i + k
            out = jnp.dot(
                uv[head],
                latent[:, k * tokens : (k + 1) * tokens],
                preferred_element_type=jnp.float32,
            )
            ho_t[pl.ds(head * vh, vh), :] = out.astype(jnp.bfloat16)
    if turn:
        for head in range(turned.shape[0]):
            turned[head] = to_turn[head].T
    if last:
        ho_out[...] = ho_t[...].T
        project_items(items, ho_out, weight_copies, weights, sent)


def start_weights(items, wo_hbm, weights, sems):
    copies, filled = [], {}
    parts = sorted({part for part, *_ in items})
    me = lax.axis_index("head")
    cols = wo_hbm.shape[1] // lax.axis_size("head")
    for n, (part, j, lo, width) in enumerate(items):
        at = filled.get(part, 0)
        filled[part] = at + width
        copies.append(
            pltpu.make_async_copy(
                wo_hbm.at[:, pl.ds(pl.multiple_of((me ^ j) * cols + lo, LANES), width)],
                weights[parts.index(part)].at[:, pl.ds(at, width)],
                sems.at[1 + n],
            )
        )
        copies[-1].start()
    return copies


def project_items(items, head_out, copies, weights, outs):
    parts = sorted({part for part, *_ in items})
    for n, part in enumerate(parts):
        widths = [width for other, _, _, width in items if other == part]
        for copy, (other, *_) in zip(copies, items):
            if other == part:
                copy.wait()
        value = jnp.dot(head_out[...], weights[n][...], preferred_element_type=jnp.float32)
        for at, width in enumerate(widths):
            outs[n][at] = value[:, at * width : (at + 1) * width].astype(jnp.bfloat16)


def weight_shapes(items, depth):
    sizes = {}
    for part, _, _, width in items:
        sizes[part] = sizes.get(part, 0) + width
    return [pltpu.VMEM((depth, sizes[part]), jnp.bfloat16) for part in sorted(sizes)]


def item_shapes(items, tokens):
    sizes = {}
    for part, _, _, size in items:
        sizes[part] = (sizes.get(part, (0, size))[0] + 1, size)
    return [in_vmem((sizes[part][0], tokens, sizes[part][1])) for part in sorted(sizes)]


def attend(spans, cached, q_t, bufs, pairs, state, lat, gather=None, turn=None, last=None):
    heads, width, tokens = q_t.shape
    items = last[2] if last else ()
    keys = sum(rows for rows, *_ in spans)
    stat = (len(pairs), 1, 2 * tokens)
    flops = 4 * len(pairs) * tokens * keys * (width + lat)
    moved = 2 * keys * width
    inputs, specs = [pin(cached, pltpu.SMEM)], [SMEM_SPEC]
    if gather:
        listed, own, core, hist = gather
        inputs += [listed, pin(own, pltpu.HBM), pin(core, pltpu.VMEM)]
        specs += [SMEM_SPEC, HBM_SPEC, VMEM_SPEC]
    vmem = [q_t, *bufs]
    for _, arrays in state:
        vmem += arrays
    if turn is not None:
        vmem.append(turn)
    scratch = [
        pltpu.VMEM((keys, width), jnp.bfloat16),
        pltpu.VMEM((lat, keys), jnp.bfloat16),
        pltpu.VMEM((keys, tokens), jnp.float32),
        pltpu.VMEM((2, keys, 2 * tokens), jnp.float32),
        pltpu.VMEM((2, keys, 2 * tokens), jnp.bfloat16),
        pltpu.SemaphoreType.DMA((1 + len(items),)),
    ]
    if gather:
        far = (hist + bufs[0].shape[0]) // 4
        scratch.append(pltpu.VMEM((far, width), jnp.bfloat16))
    if last:
        up, proj, _ = last
        vmem.append(up)
        out_shape = [in_vmem((tokens, heads * up.shape[1])), *item_shapes(items, tokens)]
        scratch.append(pltpu.VMEM((heads * up.shape[1], tokens), jnp.bfloat16))
        scratch += weight_shapes(items, proj.shape[0])
        columns = sum(size for _, _, _, size in items)
        flops += 2 * tokens * proj.shape[0] * columns
        moved += 2 * proj.shape[0] * columns
    else:
        out_shape = [
            in_vmem((len(pairs), lat, 2 * tokens), jnp.float32),
            in_vmem(stat, jnp.float32),
            in_vmem(stat, jnp.float32),
        ]
        if gather:
            out_shape += [in_vmem((hist, width)), in_vmem(packed_shape(far, width))]
        if turn is not None:
            out_shape.append(in_vmem((turn.shape[0], turn.shape[2], turn.shape[1])))
    inputs += [pin(value, pltpu.VMEM) for value in vmem]
    specs += [VMEM_SPEC] * len(vmem)
    if last:
        inputs.append(pin(proj, pltpu.HBM))
        specs.append(HBM_SPEC)
    groups = tuple(group for group, _ in state)
    sizes = tuple((buf.size // width, buf.shape[1] != width) for buf in bufs)
    cfg = (
        tuple(spans), sizes, pairs, groups, bool(gather), turn is not None, bool(last), tokens, lat,
        items,
    )
    outs = pl.pallas_call(
        functools.partial(attend_kernel, cfg),
        out_shape=out_shape,
        in_specs=specs,
        out_specs=[VMEM_SPEC] * len(out_shape),
        scratch_shapes=scratch,
        compiler_params=pltpu.CompilerParams(vmem_limit_bytes=24 << 20),
        cost_estimate=pl.CostEstimate(
            flops=flops, bytes_accessed=moved, transcendentals=2 * len(pairs) * tokens * keys
        ),
        name="attend_last" if last else "attend_gather" if gather else "attend",
    )(*inputs)
    return outs if last else ((pairs, (outs[1], outs[2], outs[0])), *outs[3:])


def project_kernel(items, head_out, wo_hbm, *refs):
    parts = len({part for part, *_ in items})
    outs, (sems, *weights) = refs[:parts], refs[parts:]
    copies = start_weights(items, wo_hbm, weights, sems)
    project_items(items, head_out, copies, weights, outs)


def project(head_out, proj, items, name):
    tokens, depth = head_out.shape
    out_shape = item_shapes(items, tokens)
    columns = sum(size for _, _, _, size in items)
    return pl.pallas_call(
        functools.partial(project_kernel, items),
        out_shape=out_shape,
        in_specs=[VMEM_SPEC, HBM_SPEC],
        out_specs=[VMEM_SPEC] * len(out_shape),
        scratch_shapes=[pltpu.SemaphoreType.DMA((1 + len(items),))]
        + weight_shapes(items, depth),
        compiler_params=pltpu.CompilerParams(vmem_limit_bytes=16 << 20),
        cost_estimate=pl.CostEstimate(
            flops=2 * tokens * depth * columns, bytes_accessed=2 * depth * columns, transcendentals=0
        ),
        name=name,
    )(pin(head_out, pltpu.VMEM), pin(proj, pltpu.HBM))


def flip_bit(value, axis, bit):
    size = lax.axis_size(axis)
    return lax.ppermute(value, axis, [(i, i ^ (1 << bit)) for i in range(size)])


def from_ahead(value, steps):
    size = lax.axis_size("ctx")
    return lax.ppermute(value, "ctx", [((i + steps) % size, i) for i in range(size)])


def add_halves(a, b):
    return (a.astype(jnp.float32) + b.astype(jnp.float32)).astype(jnp.bfloat16)


def sum_parts(kept, sent, orders):
    keeps, done, latest = list(kept), [None] * len(orders), None
    coming = [flip_bit(send, "head", order[0]) for send, order in zip(sent, orders)]
    for stage in range(len(orders[0])):
        for part, order in enumerate(orders):
            got, keep = coming[part], keeps[part]
            if latest is not None:
                got, _ = tie(got, latest)
            if stage + 1 == len(order):
                done[part] = keep[0].astype(jnp.float32) + got[0].astype(jnp.float32)
                continue
            half = keep.shape[0] // 2
            latest = add_halves(keep[half:], got[half:])
            coming[part] = flip_bit(latest, "head", order[stage + 1])
            keeps[part] = add_halves(keep[:half], got[:half])
    return done


def sum_to_owner(keep, send, order):
    for stage, bit in enumerate(order):
        got = flip_bit(send, "head", bit)
        if stage + 1 == len(order):
            return keep[0].astype(jnp.float32) + got[0].astype(jnp.float32)
        half = keep.shape[0] // 2
        send = add_halves(keep[half:], got[half:])
        keep = add_halves(keep[:half], got[:half])


def tie(*values):
    return lax.optimization_barrier(values)


def body(queries, new_latent, cache_pool, block_list, cached_lengths, w_uv, w_o):
    n_ctx = lax.axis_size("ctx")
    n_head = lax.axis_size("head")
    own = cache_pool[0]
    slots, blk, width = own.shape
    tokens = queries.shape[1]
    lat = w_uv.shape[1]
    blocks = block_list.shape[2]
    hist = blocks * blk
    part = hist // 4
    new_part = tokens // 4
    new_own = new_latent[0]
    proj = w_o.reshape(w_o.shape[0] * w_o.shape[1], w_o.shape[2])
    q_t = jnp.transpose(queries[0], (1, 2, 0))
    cols = proj.shape[1] // n_head
    pairs = tuple(range(q_t.shape[0] // 2))
    pairs_a, pairs_b = pairs[: (len(pairs) + 1) // 2], pairs[(len(pairs) + 1) // 2 :]

    def source_of(step):
        return lax.rem(lax.axis_index("ctx") + step, n_ctx)

    def piece_spans(step, flip):
        def history(cached):
            return cached - source_of(step) * hist - part * quarter_of(flip)

        def new(cached):
            ahead = (lax.axis_index("ctx") - source_of(step)) * tokens
            return ahead - new_part * quarter_of(flip)

        return [(part, False, history), (new_part, True, new)]

    own_spans = [
        (hist, False, lambda cached: cached - lax.axis_index("ctx") * hist),
        (tokens, True, lambda cached: 0),
    ]

    core = flip_bit(own, "pool", 0)
    listed = block_list[0, 0] - slots * lax.axis_index("pool")
    piece = pick_quarter(listed, own, core, new_own, blocks // 4)
    by_x = from_ahead(piece, 1)
    begun, kv_own, direct = attend(
        own_spans, cached_lengths, q_t, [new_own], pairs_a, [], lat, gather=(listed, own, core, hist)
    )
    by_x, direct, kv_own = tie(by_x, direct, kv_own)
    state = [begun]
    arrivals = []
    for step in range(1, n_ctx):
        if step > 1:
            by_x = from_ahead(piece, step)
        by_y = flip_bit(by_x, "head", 0)
        by_z = flip_bit(by_x, "head", 1)
        arrivals.append((by_x, by_y, by_z, from_ahead(direct, step)))
    if pairs_b:
        state += attend(own_spans, cached_lengths, q_t, [kv_own, new_own], pairs_b, [], lat)

    bits = n_head.bit_length() - 1
    half = n_head // 2
    if cols % LANES == 0 and n_head == 8:
        outer = 2 * cols // 7 // LANES * LANES
        orders = ((0, 2, 1), (1, 0, 2), (0, 1, 2))
        widths = (outer, cols - 2 * outer, outer)
        spans = [(sum(widths[:i]), widths[i]) for i in range(3)]
        ranked = [
            [(part, j, *spans[part]) for j in slot_order(order)] for part, order in enumerate(orders)
        ]
        early = tuple(ranked[0][half:] + ranked[1][half:])
        late = tuple(ranked[2][half:])
        keeps = tuple(item for ranks in ranked for item in ranks[:half])
    else:
        orders, early = (), ()

    up = None
    for step in range(1, n_ctx):
        by_x, *others = arrivals[step - 1]
        spans = piece_spans(step, 0)
        begun, *turned = attend(
            spans, cached_lengths, q_t, [by_x], pairs, state, lat, turn=w_uv if up is None else None
        )
        up = turned[0] if turned else up
        state = [begun]
        spans = piece_spans(step, 1) + piece_spans(step, 2) + piece_spans(step, 3)
        if step + 1 < n_ctx:
            state = attend(spans, cached_lengths, q_t, others, pairs, state, lat)
    head_out, *sent = attend(
        spans, cached_lengths, q_t, others, pairs, state, lat, last=(up, proj, early)
    )
    if orders:
        sent += project(head_out, proj, late, "project_late")
        head_out, sent[2] = tie(head_out, sent[2])
        kept = project(head_out, proj, keeps, "project_kept")
        done = sum_parts(kept, sent, orders)
        return jnp.concatenate(done, axis=1).astype(jnp.bfloat16)[None]
    partial_out = jnp.dot(head_out, proj, preferred_element_type=jnp.float32)
    blocks = jnp.transpose(partial_out.reshape(tokens, n_head, cols), (1, 0, 2)).astype(jnp.bfloat16)
    order = tuple(range(bits))
    mine = lax.axis_index("head") ^ jnp.array(slot_order(order), jnp.int32)
    blocks = jnp.take(blocks, mine, axis=0)
    return sum_to_owner(blocks[:half], blocks[half:], order).astype(jnp.bfloat16)[None]


def solution(mesh):
    in_specs = (
        P("pool", "ctx", "head", None),
        P("pool", "ctx", None),
        P("ctx", "pool", None, None),
        P("pool", "ctx", None),
        P("pool"),
        P("head", None, None),
        P("head", None, None),
    )
    out_specs = P("pool", "ctx", "head")
    return jax.shard_map(body, mesh=mesh, in_specs=in_specs, out_specs=out_specs, check_vma=False)
```

```python
import functools

import jax
import jax.numpy as jnp
from jax import lax
from jax.experimental import pallas as pl
from jax.experimental.pallas import tpu as pltpu
from jax.sharding import PartitionSpec as P

score_scale = 192.0 ** (-0.5)
log2_e = 1.4426950408889634
exp2_scale = score_scale * log2_e
neg_big = -1e30
pos_big = 3e38
LANES = 128
CHUNK = 96
ANY_SPEC = pl.BlockSpec(memory_space=pl.ANY)
HBM_SPEC = pl.BlockSpec(memory_space=pltpu.HBM)
VMEM_SPEC = pl.BlockSpec(memory_space=pltpu.VMEM)
SMEM_SPEC = pl.BlockSpec(memory_space=pltpu.SMEM)


def slot_order(order):
    bits = len(order)
    return [
        sum(((rank >> (bits - 1 - i)) & 1) << order[i] for i in range(bits))
        for rank in range(1 << bits)
    ]


def in_vmem(shape, dtype=jnp.bfloat16):
    return pltpu.VMEM(shape, dtype)


def pin(value, space):
    return pltpu.with_memory_space_constraint(value, space)


def block_place(listed, k, slots):
    slot = listed[k]
    return slot & (slots - 1), (slot >= 0) & (slot < slots)


def fetch_blocks(listed, ks, own, core, rows, sem):
    slots, blk, _ = own.shape
    targets = [rows.at[pl.ds(n * blk, blk)] for n in range(len(ks))]
    for k, target in zip(ks, targets):
        place, here = block_place(listed, k, slots)

        @pl.when(here)
        def _(place=place, target=target):
            pltpu.make_async_copy(own.at[place], target, sem).start()

    for k, target in zip(ks, targets):
        place, here = block_place(listed, k, slots)

        @pl.when(jnp.logical_not(here))
        def _(place=place, target=target):
            target[...] = core[place]

    def finish():
        for k, target in zip(ks, targets):
            place, here = block_place(listed, k, slots)

            @pl.when(here)
            def _(place=place, target=target):
                pltpu.make_async_copy(own.at[place], target, sem).wait()

    return finish


def quarter_of(flip):
    return (lax.axis_index("head") & 3) ^ flip


def packed_shape(rows, width):
    return (rows * width // LANES, LANES)


def pack(rows, packed):
    count, width = rows.shape
    whole = width // LANES
    for i in range(whole):
        packed[i * count : (i + 1) * count, :] = rows[:, i * LANES : (i + 1) * LANES]
    half = count // 2
    rest = whole * LANES
    packed[whole * count :, :] = jnp.concatenate([rows[0:half, rest:], rows[half:, rest:]], axis=1)


def unpack(packed, rows, at, count):
    width = rows.shape[1]
    whole = width // LANES
    for i in range(whole):
        rows[at : at + count, i * LANES : (i + 1) * LANES] = packed[i * count : (i + 1) * count, :]
    half = count // 2
    rest = whole * LANES
    rows[at : at + half, rest:] = packed[whole * count :, : width - rest]
    rows[at + half : at + count, rest:] = packed[whole * count :, width - rest :]


def pick_kernel(quarter, listed, own, core, new, piece, rows, sem):
    blk = own.shape[1]
    part = new.shape[0] // 4
    ks = [quarter * quarter_of(0) + j for j in range(quarter)]
    finish = fetch_blocks(listed, ks, own, core, rows, sem.at[0])
    mine = pl.ds(pl.multiple_of(quarter_of(0) * part, part), part)
    rows[pl.ds(quarter * blk, part), :] = new[mine, :]
    finish()
    pack(rows, piece)


def pick_quarter(listed, own, core, new, quarter):
    _, blk, width = own.shape
    rows = quarter * blk + new.shape[0] // 4
    return pl.pallas_call(
        functools.partial(pick_kernel, quarter),
        out_shape=in_vmem(packed_shape(rows, width)),
        in_specs=[SMEM_SPEC, HBM_SPEC, VMEM_SPEC, VMEM_SPEC],
        out_specs=VMEM_SPEC,
        scratch_shapes=[pltpu.VMEM((rows, width), jnp.bfloat16), pltpu.SemaphoreType.DMA((1,))],
        compiler_params=pltpu.CompilerParams(vmem_limit_bytes=8 << 20),
        cost_estimate=pl.CostEstimate(
            flops=0, bytes_accessed=4 * quarter * blk * width, transcendentals=0
        ),
        name="pick_quarter",
    )(listed, pin(own, pltpu.HBM), pin(core, pltpu.VMEM), pin(new, pltpu.VMEM))


def attend_kernel(cfg, *refs):
    spans, sizes, pairs, groups, gather, turn, last, tokens, lat, items = cfg
    refs = list(refs)
    take = lambda n: [refs.pop(0) for _ in range(n)]
    (cached,) = take(1)
    listed, own, core = take(3) if gather else (None, None, None)
    (q,) = take(1)
    bufs = take(len(sizes))
    state_in = {}
    for group in groups:
        m_in, l_in, acc_in = take(3)
        for at, i in enumerate(group):
            state_in[i] = (m_in, l_in, acc_in, at)
    (to_turn,) = take(1) if turn else (None,)
    if last:
        uv, wo_hbm = take(2)
        ho_out, *sent = take(1 + len({part for part, *_ in items}))
    else:
        acc, m_ref, l_ref = take(3)
        kv_out, direct = take(2) if gather else (None, None)
        (turned,) = take(1) if turn else (None,)
    kv, vt, cap, s_buf, p_buf, sems = take(6)
    (far_rows,) = take(1) if gather else (None,)
    if last:
        ho_t, *weights = refs
    keys = kv.shape[0]

    hist = 0
    if gather:
        hist, blk = kv_out.shape[0], own.shape[1]
        finish = fetch_blocks(listed, range(hist // blk), own, core, kv, sems.at[0])
    weight_copies = start_weights(items, wo_hbm, weights, sems) if last else []

    at = 0
    for rows, is_new, limit_of in spans:
        limit = limit_of(cached[0])
        row = lax.broadcasted_iota(jnp.int32, (rows, tokens), 0)
        if is_new:
            limit = lax.broadcasted_iota(jnp.int32, (rows, tokens), 1) + 1 + limit
        cap[pl.ds(at, rows), :] = jnp.where(row < limit, pos_big, neg_big)
        at += rows
    at = hist
    for buf, (rows, packed) in zip(bufs, sizes):
        if packed:
            unpack(buf, kv, at, rows)
        else:
            kv[pl.ds(at, rows), :] = buf[...]
        at += rows
    if gather:
        finish()
        for buf, size, start in ((kv, hist // 4, 0), (bufs[0], sizes[0][0] // 4, hist // 4)):
            rows = pl.ds(pl.multiple_of(quarter_of(3) * size, size), size)
            far_rows[pl.ds(start, size), :] = buf[rows, :]
        pack(far_rows, direct)
        kv_out[...] = kv[0:hist, :]

    def scores(n):
        i = pairs[n]
        q_pair = jnp.concatenate([q[2 * i], q[2 * i + 1]], axis=1)
        s_buf[n % 2] = jnp.dot(kv[...], q_pair, preferred_element_type=jnp.float32)

    def fold(x):
        return x.reshape(CHUNK // 8, 8, x.shape[1])

    scores(0)
    vt[...] = kv[:, :lat].T
    for n, i in enumerate(pairs):
        if n + 1 < len(pairs):
            scores(n + 1)
        buf, weight = s_buf.at[n % 2], p_buf.at[n % 2]
        top = jnp.full((8, 2 * tokens), -jnp.inf, jnp.float32)
        for r in range(0, keys, CHUNK):
            limits = cap[r : r + CHUNK, :]
            x = jnp.minimum(buf[r : r + CHUNK, :], jnp.concatenate([limits, limits], axis=1))
            buf[r : r + CHUNK, :] = x
            top = jnp.maximum(top, jnp.max(fold(x), axis=0))
        m = jnp.max(top, axis=0, keepdims=True)
        if state_in:
            m_in, l_in, acc_in, at = state_in[i]
            m_old, l_old, acc_old = m_in[at], l_in[at], acc_in[at]
            m = jnp.maximum(m, m_old)
        scaled = m * exp2_scale
        total = jnp.zeros((8, 2 * tokens), jnp.float32)
        for r in range(0, keys, CHUNK):
            p = jnp.exp2(buf[r : r + CHUNK, :] * exp2_scale - scaled)
            total = total + jnp.sum(fold(p), axis=0)
            weight[r : r + CHUNK, :] = p.astype(jnp.bfloat16)
        l = jnp.sum(total, axis=0, keepdims=True)
        o = jnp.dot(vt[...], weight[...], preferred_element_type=jnp.float32)
        if state_in:
            factor = jnp.exp2(m_old * exp2_scale - scaled)
            l = l + l_old * factor
            o = o + acc_old * factor
        if not last:
            m_ref[n] = m
            l_ref[n] = l
            acc[n] = o
            continue
        latent = (o * (1.0 / l)).astype(jnp.bfloat16)
        vh = uv.shape[1]
        both = uv[2 * i : 2 * i + 2].reshape(2 * vh, lat)
        out = jnp.dot(both, latent, preferred_element_type=jnp.float32).astype(jnp.bfloat16)
        for k in range(2):
            own_part = out[k * vh : (k + 1) * vh, k * tokens : (k + 1) * tokens]
            ho_t[pl.ds((2 * i + k) * vh, vh), :] = own_part
    if turn:
        for head in range(turned.shape[0]):
            turned[head] = to_turn[head].T
    if last:
        ho_out[...] = ho_t[...].T
        project_items(items, ho_out, weight_copies, weights, sent)


def start_weights(items, wo_hbm, weights, sems):
    copies, filled = [], {}
    parts = sorted({part for part, *_ in items})
    me = lax.axis_index("head")
    cols = wo_hbm.shape[1] // lax.axis_size("head")
    for n, (part, j, lo, width) in enumerate(items):
        at = filled.get(part, 0)
        filled[part] = at + width
        copies.append(
            pltpu.make_async_copy(
                wo_hbm.at[:, pl.ds(pl.multiple_of((me ^ j) * cols + lo, LANES), width)],
                weights[parts.index(part)].at[:, pl.ds(at, width)],
                sems.at[1 + n],
            )
        )
        copies[-1].start()
    return copies


def project_items(items, head_out, copies, weights, outs):
    parts = sorted({part for part, *_ in items})
    for n, part in enumerate(parts):
        widths = [width for other, _, _, width in items if other == part]
        for copy, (other, *_) in zip(copies, items):
            if other == part:
                copy.wait()
        value = jnp.dot(head_out[...], weights[n][...], preferred_element_type=jnp.float32)
        for at, width in enumerate(widths):
            outs[n][at] = value[:, at * width : (at + 1) * width].astype(jnp.bfloat16)


def weight_shapes(items, depth):
    sizes = {}
    for part, _, _, width in items:
        sizes[part] = sizes.get(part, 0) + width
    return [pltpu.VMEM((depth, sizes[part]), jnp.bfloat16) for part in sorted(sizes)]


def item_shapes(items, tokens):
    sizes = {}
    for part, _, _, size in items:
        sizes[part] = (sizes.get(part, (0, size))[0] + 1, size)
    return [in_vmem((sizes[part][0], tokens, sizes[part][1])) for part in sorted(sizes)]


def attend(spans, cached, q_t, bufs, pairs, state, lat, gather=None, turn=None, last=None):
    heads, width, tokens = q_t.shape
    items = last[2] if last else ()
    keys = sum(rows for rows, *_ in spans)
    stat = (len(pairs), 1, 2 * tokens)
    flops = 4 * len(pairs) * tokens * keys * (width + lat)
    moved = 2 * keys * width
    inputs, specs = [pin(cached, pltpu.SMEM)], [SMEM_SPEC]
    if gather:
        listed, own, core, hist = gather
        inputs += [listed, pin(own, pltpu.HBM), pin(core, pltpu.VMEM)]
        specs += [SMEM_SPEC, HBM_SPEC, VMEM_SPEC]
    vmem = [q_t, *bufs]
    for _, arrays in state:
        vmem += arrays
    if turn is not None:
        vmem.append(turn)
    scratch = [
        pltpu.VMEM((keys, width), jnp.bfloat16),
        pltpu.VMEM((lat, keys), jnp.bfloat16),
        pltpu.VMEM((keys, tokens), jnp.float32),
        pltpu.VMEM((2, keys, 2 * tokens), jnp.float32),
        pltpu.VMEM((2, keys, 2 * tokens), jnp.bfloat16),
        pltpu.SemaphoreType.DMA((1 + len(items),)),
    ]
    if gather:
        far = (hist + bufs[0].shape[0]) // 4
        scratch.append(pltpu.VMEM((far, width), jnp.bfloat16))
    if last:
        up, proj, _ = last
        vmem.append(up)
        out_shape = [in_vmem((tokens, heads * up.shape[1])), *item_shapes(items, tokens)]
        scratch.append(pltpu.VMEM((heads * up.shape[1], tokens), jnp.bfloat16))
        scratch += weight_shapes(items, proj.shape[0])
        columns = sum(size for _, _, _, size in items)
        flops += 2 * tokens * proj.shape[0] * columns
        moved += 2 * proj.shape[0] * columns
    else:
        out_shape = [
            in_vmem((len(pairs), lat, 2 * tokens), jnp.float32),
            in_vmem(stat, jnp.float32),
            in_vmem(stat, jnp.float32),
        ]
        if gather:
            out_shape += [in_vmem((hist, width)), in_vmem(packed_shape(far, width))]
        if turn is not None:
            out_shape.append(in_vmem((turn.shape[0], turn.shape[2], turn.shape[1])))
    inputs += [pin(value, pltpu.VMEM) for value in vmem]
    specs += [VMEM_SPEC] * len(vmem)
    if last:
        inputs.append(pin(proj, pltpu.HBM))
        specs.append(HBM_SPEC)
    groups = tuple(group for group, _ in state)
    sizes = tuple((buf.size // width, buf.shape[1] != width) for buf in bufs)
    cfg = (
        tuple(spans), sizes, pairs, groups, bool(gather), turn is not None, bool(last), tokens, lat,
        items,
    )
    outs = pl.pallas_call(
        functools.partial(attend_kernel, cfg),
        out_shape=out_shape,
        in_specs=specs,
        out_specs=[VMEM_SPEC] * len(out_shape),
        scratch_shapes=scratch,
        compiler_params=pltpu.CompilerParams(vmem_limit_bytes=24 << 20),
        cost_estimate=pl.CostEstimate(
            flops=flops, bytes_accessed=moved, transcendentals=2 * len(pairs) * tokens * keys
        ),
        name="attend_last" if last else "attend_gather" if gather else "attend",
    )(*inputs)
    return outs if last else ((pairs, (outs[1], outs[2], outs[0])), *outs[3:])


def project_kernel(items, head_out, wo_hbm, *refs):
    parts = len({part for part, *_ in items})
    outs, (sems, *weights) = refs[:parts], refs[parts:]
    copies = start_weights(items, wo_hbm, weights, sems)
    project_items(items, head_out, copies, weights, outs)


def project(head_out, proj, items, name):
    tokens, depth = head_out.shape
    out_shape = item_shapes(items, tokens)
    columns = sum(size for _, _, _, size in items)
    return pl.pallas_call(
        functools.partial(project_kernel, items),
        out_shape=out_shape,
        in_specs=[VMEM_SPEC, HBM_SPEC],
        out_specs=[VMEM_SPEC] * len(out_shape),
        scratch_shapes=[pltpu.SemaphoreType.DMA((1 + len(items),))]
        + weight_shapes(items, depth),
        compiler_params=pltpu.CompilerParams(vmem_limit_bytes=16 << 20),
        cost_estimate=pl.CostEstimate(
            flops=2 * tokens * depth * columns, bytes_accessed=2 * depth * columns, transcendentals=0
        ),
        name=name,
    )(pin(head_out, pltpu.VMEM), pin(proj, pltpu.HBM))


def flip_bit(value, axis, bit):
    size = lax.axis_size(axis)
    return lax.ppermute(value, axis, [(i, i ^ (1 << bit)) for i in range(size)])


def from_ahead(value, steps):
    size = lax.axis_size("ctx")
    return lax.ppermute(value, "ctx", [((i + steps) % size, i) for i in range(size)])


def add_halves(a, b):
    return (a.astype(jnp.float32) + b.astype(jnp.float32)).astype(jnp.bfloat16)


def sum_parts(kept, sent, orders):
    keeps, done, latest = list(kept), [None] * len(orders), None
    coming = [flip_bit(send, "head", order[0]) for send, order in zip(sent, orders)]
    for stage in range(len(orders[0])):
        for part, order in enumerate(orders):
            got, keep = coming[part], keeps[part]
            if latest is not None:
                got, _ = tie(got, latest)
            if stage + 1 == len(order):
                done[part] = keep[0].astype(jnp.float32) + got[0].astype(jnp.float32)
                continue
            half = keep.shape[0] // 2
            latest = add_halves(keep[half:], got[half:])
            coming[part] = flip_bit(latest, "head", order[stage + 1])
            keeps[part] = add_halves(keep[:half], got[:half])
    return done


def sum_to_owner(keep, send, order):
    for stage, bit in enumerate(order):
        got = flip_bit(send, "head", bit)
        if stage + 1 == len(order):
            return keep[0].astype(jnp.float32) + got[0].astype(jnp.float32)
        half = keep.shape[0] // 2
        send = add_halves(keep[half:], got[half:])
        keep = add_halves(keep[:half], got[:half])


def tie(*values):
    return lax.optimization_barrier(values)


def body(queries, new_latent, cache_pool, block_list, cached_lengths, w_uv, w_o):
    n_ctx = lax.axis_size("ctx")
    n_head = lax.axis_size("head")
    own = cache_pool[0]
    slots, blk, width = own.shape
    tokens = queries.shape[1]
    lat = w_uv.shape[1]
    blocks = block_list.shape[2]
    hist = blocks * blk
    part = hist // 4
    new_part = tokens // 4
    new_own = new_latent[0]
    proj = w_o.reshape(w_o.shape[0] * w_o.shape[1], w_o.shape[2])
    q_t = jnp.transpose(queries[0], (1, 2, 0))
    cols = proj.shape[1] // n_head
    pairs = tuple(range(q_t.shape[0] // 2))
    pairs_a, pairs_b = pairs[: (len(pairs) + 1) // 2], pairs[(len(pairs) + 1) // 2 :]

    def source_of(step):
        return lax.rem(lax.axis_index("ctx") + step, n_ctx)

    def piece_spans(step, flip):
        def history(cached):
            return cached - source_of(step) * hist - part * quarter_of(flip)

        def new(cached):
            ahead = (lax.axis_index("ctx") - source_of(step)) * tokens
            return ahead - new_part * quarter_of(flip)

        return [(part, False, history), (new_part, True, new)]

    own_spans = [
        (hist, False, lambda cached: cached - lax.axis_index("ctx") * hist),
        (tokens, True, lambda cached: 0),
    ]

    core = flip_bit(own, "pool", 0)
    listed = block_list[0, 0] - slots * lax.axis_index("pool")
    piece = pick_quarter(listed, own, core, new_own, blocks // 4)
    by_x = from_ahead(piece, 1)
    begun, kv_own, direct = attend(
        own_spans, cached_lengths, q_t, [new_own], pairs_a, [], lat, gather=(listed, own, core, hist)
    )
    by_x, direct, kv_own = tie(by_x, direct, kv_own)
    state = [begun]
    arrivals = []
    for step in range(1, n_ctx):
        if step > 1:
            by_x = from_ahead(piece, step)
        by_y = flip_bit(by_x, "head", 0)
        by_z = flip_bit(by_x, "head", 1)
        arrivals.append((by_x, by_y, by_z, from_ahead(direct, step)))
    if pairs_b:
        state += attend(own_spans, cached_lengths, q_t, [kv_own, new_own], pairs_b, [], lat)

    bits = n_head.bit_length() - 1
    half = n_head // 2
    if cols % LANES == 0 and n_head == 8:
        outer = 2 * cols // 7 // LANES * LANES
        orders = ((0, 1, 2), (1, 0, 2), (0, 1, 2))
        widths = (outer, cols - 2 * outer, outer)
        spans = [(sum(widths[:i]), widths[i]) for i in range(3)]
        ranked = [
            [(part, j, *spans[part]) for j in slot_order(order)] for part, order in enumerate(orders)
        ]
        early = tuple(ranked[0][half:] + ranked[1][half:])
        late = tuple(ranked[2][half:])
        keeps = tuple(item for ranks in ranked for item in ranks[:half])
    else:
        orders, early = (), ()

    up = None
    for step in range(1, n_ctx):
        by_x, *others = arrivals[step - 1]
        spans = piece_spans(step, 0)
        begun, *turned = attend(
            spans, cached_lengths, q_t, [by_x], pairs, state, lat, turn=w_uv if up is None else None
        )
        up = turned[0] if turned else up
        state = [begun]
        spans = piece_spans(step, 1) + piece_spans(step, 2) + piece_spans(step, 3)
        if step + 1 < n_ctx:
            state = attend(spans, cached_lengths, q_t, others, pairs, state, lat)
    head_out, *sent = attend(
        spans, cached_lengths, q_t, others, pairs, state, lat, last=(up, proj, early)
    )
    if orders:
        sent += project(head_out, proj, late, "project_late")
        head_out, sent[2] = tie(head_out, sent[2])
        kept = project(head_out, proj, keeps, "project_kept")
        done = sum_parts(kept, sent, orders)
        return jnp.concatenate(done, axis=1).astype(jnp.bfloat16)[None]
    partial_out = jnp.dot(head_out, proj, preferred_element_type=jnp.float32)
    blocks = jnp.transpose(partial_out.reshape(tokens, n_head, cols), (1, 0, 2)).astype(jnp.bfloat16)
    order = tuple(range(bits))
    mine = lax.axis_index("head") ^ jnp.array(slot_order(order), jnp.int32)
    blocks = jnp.take(blocks, mine, axis=0)
    return sum_to_owner(blocks[:half], blocks[half:], order).astype(jnp.bfloat16)[None]


def solution(mesh):
    in_specs = (
        P("pool", "ctx", "head", None),
        P("pool", "ctx", None),
        P("ctx", "pool", None, None),
        P("pool", "ctx", None),
        P("pool"),
        P("head", None, None),
        P("head", None, None),
    )
    out_specs = P("pool", "ctx", "head")
    return jax.shard_map(body, mesh=mesh, in_specs=in_specs, out_specs=out_specs, check_vma=False)
```

```python
import functools

import jax
import jax.numpy as jnp
from jax import lax
from jax.experimental import pallas as pl
from jax.experimental.pallas import tpu as pltpu
from jax.sharding import PartitionSpec as P

score_scale = 192.0 ** (-0.5)
log2_e = 1.4426950408889634
exp2_scale = score_scale * log2_e
neg_big = -1e30
pos_big = 3e38
LANES = 128
CHUNK = 96
ANY_SPEC = pl.BlockSpec(memory_space=pl.ANY)
HBM_SPEC = pl.BlockSpec(memory_space=pltpu.HBM)
VMEM_SPEC = pl.BlockSpec(memory_space=pltpu.VMEM)
SMEM_SPEC = pl.BlockSpec(memory_space=pltpu.SMEM)


def slot_order(order):
    bits = len(order)
    return [
        sum(((rank >> (bits - 1 - i)) & 1) << order[i] for i in range(bits))
        for rank in range(1 << bits)
    ]


def in_vmem(shape, dtype=jnp.bfloat16):
    return pltpu.VMEM(shape, dtype)


def pin(value, space):
    return pltpu.with_memory_space_constraint(value, space)


def block_place(listed, k, slots):
    slot = listed[k]
    return slot & (slots - 1), (slot >= 0) & (slot < slots)


def fetch_blocks(listed, ks, own, core, rows):
    slots, blk, _ = own.shape
    for n, k in enumerate(ks):
        place, here = block_place(listed, k, slots)
        target = rows.at[pl.ds(n * blk, blk)]

        @pl.when(here)
        def _(place=place, target=target):
            target[...] = own[place]

        @pl.when(jnp.logical_not(here))
        def _(place=place, target=target):
            target[...] = core[place]


def stage_kernel(pool, new_t, own, new, turned, sems):
    copies = [
        pltpu.make_async_copy(new_t, turned, sems.at[0]),
        pltpu.make_async_copy(pool, own, sems.at[1]),
    ]
    for copy in copies:
        copy.start()
    copies[0].wait()
    new[...] = turned[...].T
    copies[1].wait()


def stage(pool, new_t):
    return pl.pallas_call(
        stage_kernel,
        out_shape=[in_vmem(pool.shape), in_vmem(new_t.shape[::-1])],
        in_specs=[HBM_SPEC, HBM_SPEC],
        out_specs=[VMEM_SPEC, VMEM_SPEC],
        scratch_shapes=[pltpu.VMEM(new_t.shape, jnp.bfloat16), pltpu.SemaphoreType.DMA((2,))],
        compiler_params=pltpu.CompilerParams(vmem_limit_bytes=8 << 20),
        cost_estimate=pl.CostEstimate(flops=0, bytes_accessed=4 * pool.size, transcendentals=0),
        name="stage",
    )(pin(pool, pltpu.HBM), pin(new_t, pltpu.HBM))


def quarter_of(flip):
    return (lax.axis_index("head") & 3) ^ flip


def packed_shape(rows, width):
    return (rows * width // LANES, LANES)


def pack(rows, packed):
    count, width = rows.shape
    whole = width // LANES
    for i in range(whole):
        packed[i * count : (i + 1) * count, :] = rows[:, i * LANES : (i + 1) * LANES]
    half = count // 2
    rest = whole * LANES
    packed[whole * count :, :] = jnp.concatenate([rows[0:half, rest:], rows[half:, rest:]], axis=1)


def unpack(packed, rows, at, count):
    width = rows.shape[1]
    whole = width // LANES
    for i in range(whole):
        rows[at : at + count, i * LANES : (i + 1) * LANES] = packed[i * count : (i + 1) * count, :]
    half = count // 2
    rest = whole * LANES
    rows[at : at + half, rest:] = packed[whole * count :, : width - rest]
    rows[at + half : at + count, rest:] = packed[whole * count :, width - rest :]


def pick_kernel(quarter, listed, own, core, new, piece, rows):
    blk = own.shape[1]
    part = new.shape[0] // 4
    ks = [quarter * quarter_of(0) + j for j in range(quarter)]
    fetch_blocks(listed, ks, own, core, rows)
    mine = pl.ds(pl.multiple_of(quarter_of(0) * part, part), part)
    rows[pl.ds(quarter * blk, part), :] = new[mine, :]
    pack(rows, piece)


def pick_quarter(listed, own, core, new, quarter):
    _, blk, width = own.shape
    rows = quarter * blk + new.shape[0] // 4
    return pl.pallas_call(
        functools.partial(pick_kernel, quarter),
        out_shape=in_vmem(packed_shape(rows, width)),
        in_specs=[SMEM_SPEC, VMEM_SPEC, VMEM_SPEC, VMEM_SPEC],
        out_specs=VMEM_SPEC,
        scratch_shapes=[pltpu.VMEM((rows, width), jnp.bfloat16)],
        compiler_params=pltpu.CompilerParams(vmem_limit_bytes=8 << 20),
        cost_estimate=pl.CostEstimate(
            flops=0, bytes_accessed=4 * quarter * blk * width, transcendentals=0
        ),
        name="pick_quarter",
    )(listed, *[pin(value, pltpu.VMEM) for value in (own, core, new)])


def attend_kernel(cfg, *refs):
    spans, sizes, pairs, groups, gather, turn, last, tokens, lat, items = cfg
    refs = list(refs)
    take = lambda n: [refs.pop(0) for _ in range(n)]
    (cached,) = take(1)
    listed, own, core = take(3) if gather else (None, None, None)
    (q,) = take(1)
    bufs = take(len(sizes))
    state_in = {}
    for group in groups:
        m_in, l_in, acc_in = take(3)
        for at, i in enumerate(group):
            state_in[i] = (m_in, l_in, acc_in, at)
    (to_turn,) = take(1) if turn else (None,)
    if last:
        uv, wo_hbm = take(2)
        ho_out, *sent = take(1 + len({part for part, *_ in items}))
    else:
        acc, m_ref, l_ref = take(3)
        kv_out, direct = take(2) if gather else (None, None)
        (turned,) = take(1) if turn else (None,)
    kv, vt, cap, s_buf, p_buf, sems = take(6)
    (far_rows,) = take(1) if gather else (None,)
    if last:
        ho_t, *weights = refs
    keys = kv.shape[0]

    hist = 0
    if gather:
        hist, blk = kv_out.shape[0], own.shape[1]
        fetch_blocks(listed, range(hist // blk), own, core, kv)
    weight_copies = start_weights(items, wo_hbm, weights, sems) if last else []

    at = 0
    for rows, is_new, limit_of in spans:
        limit = limit_of(cached[0])
        row = lax.broadcasted_iota(jnp.int32, (rows, tokens), 0)
        if is_new:
            limit = lax.broadcasted_iota(jnp.int32, (rows, tokens), 1) + 1 + limit
        cap[pl.ds(at, rows), :] = jnp.where(row < limit, pos_big, neg_big)
        at += rows
    at = hist
    for buf, (rows, packed) in zip(bufs, sizes):
        if packed:
            unpack(buf, kv, at, rows)
        else:
            kv[pl.ds(at, rows), :] = buf[...]
        at += rows
    if gather:
        for buf, size, start in ((kv, hist // 4, 0), (bufs[0], sizes[0][0] // 4, hist // 4)):
            rows = pl.ds(pl.multiple_of(quarter_of(3) * size, size), size)
            far_rows[pl.ds(start, size), :] = buf[rows, :]
        pack(far_rows, direct)
        kv_out[...] = kv[0:hist, :]

    def scores(n):
        i = pairs[n]
        q_pair = jnp.concatenate([q[2 * i], q[2 * i + 1]], axis=1)
        s_buf[n % 2] = jnp.dot(kv[...], q_pair, preferred_element_type=jnp.float32)

    def fold(x):
        return x.reshape(CHUNK // 8, 8, x.shape[1])

    scores(0)
    vt[...] = kv[:, :lat].T
    for n, i in enumerate(pairs):
        if n + 1 < len(pairs):
            scores(n + 1)
        buf, weight = s_buf.at[n % 2], p_buf.at[n % 2]
        top = jnp.full((8, 2 * tokens), -jnp.inf, jnp.float32)
        for r in range(0, keys, CHUNK):
            limits = cap[r : r + CHUNK, :]
            x = jnp.minimum(buf[r : r + CHUNK, :], jnp.concatenate([limits, limits], axis=1))
            buf[r : r + CHUNK, :] = x
            top = jnp.maximum(top, jnp.max(fold(x), axis=0))
        m = jnp.max(top, axis=0, keepdims=True)
        if state_in:
            m_in, l_in, acc_in, at = state_in[i]
            m_old, l_old, acc_old = m_in[at], l_in[at], acc_in[at]
            m = jnp.maximum(m, m_old)
        scaled = m * exp2_scale
        total = jnp.zeros((8, 2 * tokens), jnp.float32)
        for r in range(0, keys, CHUNK):
            p = jnp.exp2(buf[r : r + CHUNK, :] * exp2_scale - scaled)
            total = total + jnp.sum(fold(p), axis=0)
            weight[r : r + CHUNK, :] = p.astype(jnp.bfloat16)
        l = jnp.sum(total, axis=0, keepdims=True)
        o = jnp.dot(vt[...], weight[...], preferred_element_type=jnp.float32)
        if state_in:
            factor = jnp.exp2(m_old * exp2_scale - scaled)
            l = l + l_old * factor
            o = o + acc_old * factor
        if not last:
            m_ref[n] = m
            l_ref[n] = l
            acc[n] = o
            continue
        latent = (o * (1.0 / l)).astype(jnp.bfloat16)
        vh = uv.shape[1]
        both = uv[2 * i : 2 * i + 2].reshape(2 * vh, lat)
        out = jnp.dot(both, latent, preferred_element_type=jnp.float32).astype(jnp.bfloat16)
        for k in range(2):
            own_part = out[k * vh : (k + 1) * vh, k * tokens : (k + 1) * tokens]
            ho_t[pl.ds((2 * i + k) * vh, vh), :] = own_part
    if turn:
        for head in range(turned.shape[0]):
            turned[head] = to_turn[head].T
    if last:
        ho_out[...] = ho_t[...].T
        project_items(items, ho_out, weight_copies, weights, sent)


def start_weights(items, wo_hbm, weights, sems):
    copies, filled = [], {}
    parts = sorted({part for part, *_ in items})
    me = lax.axis_index("head")
    cols = wo_hbm.shape[1] // lax.axis_size("head")
    for n, (part, j, lo, width) in enumerate(items):
        at = filled.get(part, 0)
        filled[part] = at + width
        copies.append(
            pltpu.make_async_copy(
                wo_hbm.at[:, pl.ds(pl.multiple_of((me ^ j) * cols + lo, LANES), width)],
                weights[parts.index(part)].at[:, pl.ds(at, width)],
                sems.at[1 + n],
            )
        )
        copies[-1].start()
    return copies


def project_items(items, head_out, copies, weights, outs):
    parts = sorted({part for part, *_ in items})
    for n, part in enumerate(parts):
        widths = [width for other, _, _, width in items if other == part]
        for copy, (other, *_) in zip(copies, items):
            if other == part:
                copy.wait()
        value = jnp.dot(head_out[...], weights[n][...], preferred_element_type=jnp.float32)
        for at, width in enumerate(widths):
            outs[n][at] = value[:, at * width : (at + 1) * width].astype(jnp.bfloat16)


def weight_shapes(items, depth):
    sizes = {}
    for part, _, _, width in items:
        sizes[part] = sizes.get(part, 0) + width
    return [pltpu.VMEM((depth, sizes[part]), jnp.bfloat16) for part in sorted(sizes)]


def item_shapes(items, tokens):
    sizes = {}
    for part, _, _, size in items:
        sizes[part] = (sizes.get(part, (0, size))[0] + 1, size)
    return [in_vmem((sizes[part][0], tokens, sizes[part][1])) for part in sorted(sizes)]


def attend(spans, cached, q_t, bufs, pairs, state, lat, gather=None, turn=None, last=None):
    heads, width, tokens = q_t.shape
    items = last[2] if last else ()
    keys = sum(rows for rows, *_ in spans)
    stat = (len(pairs), 1, 2 * tokens)
    flops = 4 * len(pairs) * tokens * keys * (width + lat)
    moved = 2 * keys * width
    inputs, specs = [pin(cached, pltpu.SMEM)], [SMEM_SPEC]
    if gather:
        listed, own, core, hist = gather
        inputs += [listed, pin(own, pltpu.VMEM), pin(core, pltpu.VMEM)]
        specs += [SMEM_SPEC, VMEM_SPEC, VMEM_SPEC]
    vmem = [q_t, *bufs]
    for _, arrays in state:
        vmem += arrays
    if turn is not None:
        vmem.append(turn)
    scratch = [
        pltpu.VMEM((keys, width), jnp.bfloat16),
        pltpu.VMEM((lat, keys), jnp.bfloat16),
        pltpu.VMEM((keys, tokens), jnp.float32),
        pltpu.VMEM((2, keys, 2 * tokens), jnp.float32),
        pltpu.VMEM((2, keys, 2 * tokens), jnp.bfloat16),
        pltpu.SemaphoreType.DMA((1 + len(items),)),
    ]
    if gather:
        far = (hist + bufs[0].shape[0]) // 4
        scratch.append(pltpu.VMEM((far, width), jnp.bfloat16))
    if last:
        up, proj, _ = last
        vmem.append(up)
        out_shape = [in_vmem((tokens, heads * up.shape[1])), *item_shapes(items, tokens)]
        scratch.append(pltpu.VMEM((heads * up.shape[1], tokens), jnp.bfloat16))
        scratch += weight_shapes(items, proj.shape[0])
        columns = sum(size for _, _, _, size in items)
        flops += 2 * tokens * proj.shape[0] * columns
        moved += 2 * proj.shape[0] * columns
    else:
        out_shape = [
            in_vmem((len(pairs), lat, 2 * tokens), jnp.float32),
            in_vmem(stat, jnp.float32),
            in_vmem(stat, jnp.float32),
        ]
        if gather:
            out_shape += [in_vmem((hist, width)), in_vmem(packed_shape(far, width))]
        if turn is not None:
            out_shape.append(in_vmem((turn.shape[0], turn.shape[2], turn.shape[1])))
    inputs += [pin(value, pltpu.VMEM) for value in vmem]
    specs += [VMEM_SPEC] * len(vmem)
    if last:
        inputs.append(pin(proj, pltpu.HBM))
        specs.append(HBM_SPEC)
    groups = tuple(group for group, _ in state)
    sizes = tuple((buf.size // width, buf.shape[1] != width) for buf in bufs)
    cfg = (
        tuple(spans), sizes, pairs, groups, bool(gather), turn is not None, bool(last), tokens, lat,
        items,
    )
    outs = pl.pallas_call(
        functools.partial(attend_kernel, cfg),
        out_shape=out_shape,
        in_specs=specs,
        out_specs=[VMEM_SPEC] * len(out_shape),
        scratch_shapes=scratch,
        compiler_params=pltpu.CompilerParams(vmem_limit_bytes=24 << 20),
        cost_estimate=pl.CostEstimate(
            flops=flops, bytes_accessed=moved, transcendentals=2 * len(pairs) * tokens * keys
        ),
        name="attend_last" if last else "attend_gather" if gather else "attend",
    )(*inputs)
    return outs if last else ((pairs, (outs[1], outs[2], outs[0])), *outs[3:])


def project_kernel(items, head_out, wo_hbm, *refs):
    parts = len({part for part, *_ in items})
    outs, (sems, *weights) = refs[:parts], refs[parts:]
    copies = start_weights(items, wo_hbm, weights, sems)
    project_items(items, head_out, copies, weights, outs)


def project(head_out, proj, items, name):
    tokens, depth = head_out.shape
    out_shape = item_shapes(items, tokens)
    columns = sum(size for _, _, _, size in items)
    return pl.pallas_call(
        functools.partial(project_kernel, items),
        out_shape=out_shape,
        in_specs=[VMEM_SPEC, HBM_SPEC],
        out_specs=[VMEM_SPEC] * len(out_shape),
        scratch_shapes=[pltpu.SemaphoreType.DMA((1 + len(items),))]
        + weight_shapes(items, depth),
        compiler_params=pltpu.CompilerParams(vmem_limit_bytes=16 << 20),
        cost_estimate=pl.CostEstimate(
            flops=2 * tokens * depth * columns, bytes_accessed=2 * depth * columns, transcendentals=0
        ),
        name=name,
    )(pin(head_out, pltpu.VMEM), pin(proj, pltpu.HBM))


def flip_bit(value, axis, bit):
    size = lax.axis_size(axis)
    return lax.ppermute(value, axis, [(i, i ^ (1 << bit)) for i in range(size)])


def from_ahead(value, steps):
    size = lax.axis_size("ctx")
    return lax.ppermute(value, "ctx", [((i + steps) % size, i) for i in range(size)])


def add_halves(a, b):
    return (a.astype(jnp.float32) + b.astype(jnp.float32)).astype(jnp.bfloat16)


def sum_parts(kept, sent, orders):
    keeps, done, latest = list(kept), [None] * len(orders), None
    coming = [flip_bit(send, "head", order[0]) for send, order in zip(sent, orders)]
    for stage in range(len(orders[0])):
        for part, order in enumerate(orders):
            got, keep = coming[part], keeps[part]
            if latest is not None:
                got, _ = tie(got, latest)
            if stage + 1 == len(order):
                done[part] = keep[0].astype(jnp.float32) + got[0].astype(jnp.float32)
                continue
            half = keep.shape[0] // 2
            latest = add_halves(keep[half:], got[half:])
            coming[part] = flip_bit(latest, "head", order[stage + 1])
            keeps[part] = add_halves(keep[:half], got[:half])
    return done


def sum_to_owner(keep, send, order):
    for stage, bit in enumerate(order):
        got = flip_bit(send, "head", bit)
        if stage + 1 == len(order):
            return keep[0].astype(jnp.float32) + got[0].astype(jnp.float32)
        half = keep.shape[0] // 2
        send = add_halves(keep[half:], got[half:])
        keep = add_halves(keep[:half], got[:half])


def tie(*values):
    return lax.optimization_barrier(values)


def body(queries, new_latent, cache_pool, block_list, cached_lengths, w_uv, w_o):
    n_ctx = lax.axis_size("ctx")
    n_head = lax.axis_size("head")
    pool = cache_pool[0]
    slots, blk, width = pool.shape
    tokens = queries.shape[1]
    lat = w_uv.shape[1]
    blocks = block_list.shape[2]
    hist = blocks * blk
    part = hist // 4
    new_part = tokens // 4
    proj = w_o.reshape(w_o.shape[0] * w_o.shape[1], w_o.shape[2])
    q_t = jnp.transpose(queries[0], (1, 2, 0))
    cols = proj.shape[1] // n_head
    pairs = tuple(range(q_t.shape[0] // 2))
    pairs_a, pairs_b = pairs[: (len(pairs) + 1) // 2], pairs[(len(pairs) + 1) // 2 :]

    def source_of(step):
        return lax.rem(lax.axis_index("ctx") + step, n_ctx)

    def piece_spans(step, flip):
        def history(cached):
            return cached - source_of(step) * hist - part * quarter_of(flip)

        def new(cached):
            ahead = (lax.axis_index("ctx") - source_of(step)) * tokens
            return ahead - new_part * quarter_of(flip)

        return [(part, False, history), (new_part, True, new)]

    own_spans = [
        (hist, False, lambda cached: cached - lax.axis_index("ctx") * hist),
        (tokens, True, lambda cached: 0),
    ]

    core = flip_bit(pool, "pool", 0)
    own, new_own = stage(pool, jnp.transpose(new_latent[0], (1, 0)))
    listed = block_list[0, 0] - slots * lax.axis_index("pool")
    piece = pick_quarter(listed, own, core, new_own, blocks // 4)
    by_x = from_ahead(piece, 1)
    begun, kv_own, direct = attend(
        own_spans, cached_lengths, q_t, [new_own], pairs_a, [], lat, gather=(listed, own, core, hist)
    )
    by_x, direct, kv_own = tie(by_x, direct, kv_own)
    state = [begun]
    arrivals = []
    for step in range(1, n_ctx):
        if step > 1:
            by_x = from_ahead(piece, step)
        by_y = flip_bit(by_x, "head", 0)
        by_z = flip_bit(by_x, "head", 1)
        arrivals.append((by_x, by_y, by_z, from_ahead(direct, step)))
    if pairs_b:
        state += attend(own_spans, cached_lengths, q_t, [kv_own, new_own], pairs_b, [], lat)

    bits = n_head.bit_length() - 1
    half = n_head // 2
    if cols % LANES == 0 and n_head == 8:
        outer = 2 * cols // 7 // LANES * LANES
        orders = ((0, 1, 2), (1, 0, 2), (0, 1, 2))
        widths = (outer, cols - 2 * outer, outer)
        spans = [(sum(widths[:i]), widths[i]) for i in range(3)]
        ranked = [
            [(part, j, *spans[part]) for j in slot_order(order)] for part, order in enumerate(orders)
        ]
        early = tuple(ranked[0][half:] + ranked[1][half:])
        late = tuple(ranked[2][half:])
        keeps = tuple(item for ranks in ranked for item in ranks[:half])
    else:
        orders, early = (), ()

    up = None
    for step in range(1, n_ctx):
        by_x, *others = arrivals[step - 1]
        spans = piece_spans(step, 0)
        begun, *turned = attend(
            spans, cached_lengths, q_t, [by_x], pairs, state, lat, turn=w_uv if up is None else None
        )
        up = turned[0] if turned else up
        state = [begun]
        spans = piece_spans(step, 1) + piece_spans(step, 2) + piece_spans(step, 3)
        if step + 1 < n_ctx:
            state = attend(spans, cached_lengths, q_t, others, pairs, state, lat)
    head_out, *sent = attend(
        spans, cached_lengths, q_t, others, pairs, state, lat, last=(up, proj, early)
    )
    if orders:
        sent += project(head_out, proj, late, "project_late")
        head_out, sent[2] = tie(head_out, sent[2])
        kept = project(head_out, proj, keeps, "project_kept")
        done = sum_parts(kept, sent, orders)
        return jnp.concatenate(done, axis=1).astype(jnp.bfloat16)[None]
    partial_out = jnp.dot(head_out, proj, preferred_element_type=jnp.float32)
    blocks = jnp.transpose(partial_out.reshape(tokens, n_head, cols), (1, 0, 2)).astype(jnp.bfloat16)
    order = tuple(range(bits))
    mine = lax.axis_index("head") ^ jnp.array(slot_order(order), jnp.int32)
    blocks = jnp.take(blocks, mine, axis=0)
    return sum_to_owner(blocks[:half], blocks[half:], order).astype(jnp.bfloat16)[None]


def solution(mesh):
    in_specs = (
        P("pool", "ctx", "head", None),
        P("pool", "ctx", None),
        P("ctx", "pool", None, None),
        P("pool", "ctx", None),
        P("pool"),
        P("head", None, None),
        P("head", None, None),
    )
    out_specs = P("pool", "ctx", "head")
    return jax.shard_map(body, mesh=mesh, in_specs=in_specs, out_specs=out_specs, check_vma=False)
```

```python
import functools

import jax
import jax.numpy as jnp
from jax import lax
from jax.experimental import pallas as pl
from jax.experimental.pallas import tpu as pltpu
from jax.sharding import PartitionSpec as P

score_scale = 192.0 ** (-0.5)
log2_e = 1.4426950408889634
exp2_scale = score_scale * log2_e
neg_big = -1e30
pos_big = 3e38
LANES = 128
CHUNK = 48
ANY_SPEC = pl.BlockSpec(memory_space=pl.ANY)
HBM_SPEC = pl.BlockSpec(memory_space=pltpu.HBM)
VMEM_SPEC = pl.BlockSpec(memory_space=pltpu.VMEM)
SMEM_SPEC = pl.BlockSpec(memory_space=pltpu.SMEM)


def slot_order(order):
    bits = len(order)
    return [
        sum(((rank >> (bits - 1 - i)) & 1) << order[i] for i in range(bits))
        for rank in range(1 << bits)
    ]


def in_vmem(shape, dtype=jnp.bfloat16):
    return pltpu.VMEM(shape, dtype)


def pin(value, space):
    return pltpu.with_memory_space_constraint(value, space)


def block_place(listed, k, slots):
    slot = listed[k]
    return slot & (slots - 1), (slot >= 0) & (slot < slots)


def fetch_blocks(listed, ks, own, core, rows):
    slots, blk, _ = own.shape
    for n, k in enumerate(ks):
        place, here = block_place(listed, k, slots)
        target = rows.at[pl.ds(n * blk, blk)]

        @pl.when(here)
        def _(place=place, target=target):
            target[...] = own[place]

        @pl.when(jnp.logical_not(here))
        def _(place=place, target=target):
            target[...] = core[place]


def stage_kernel(pool, new_t, own, new, turned, sems):
    copies = [
        pltpu.make_async_copy(new_t, turned, sems.at[0]),
        pltpu.make_async_copy(pool, own, sems.at[1]),
    ]
    for copy in copies:
        copy.start()
    copies[0].wait()
    new[...] = turned[...].T
    copies[1].wait()


def stage(pool, new_t):
    return pl.pallas_call(
        stage_kernel,
        out_shape=[in_vmem(pool.shape), in_vmem(new_t.shape[::-1])],
        in_specs=[HBM_SPEC, HBM_SPEC],
        out_specs=[VMEM_SPEC, VMEM_SPEC],
        scratch_shapes=[pltpu.VMEM(new_t.shape, jnp.bfloat16), pltpu.SemaphoreType.DMA((2,))],
        compiler_params=pltpu.CompilerParams(vmem_limit_bytes=8 << 20),
        cost_estimate=pl.CostEstimate(flops=0, bytes_accessed=4 * pool.size, transcendentals=0),
        name="stage",
    )(pin(pool, pltpu.HBM), pin(new_t, pltpu.HBM))


def quarter_of(flip):
    return (lax.axis_index("head") & 3) ^ flip


def packed_shape(rows, width):
    return (rows * width // LANES, LANES)


def pack(rows, packed):
    count, width = rows.shape
    whole = width // LANES
    for i in range(whole):
        packed[i * count : (i + 1) * count, :] = rows[:, i * LANES : (i + 1) * LANES]
    half = count // 2
    rest = whole * LANES
    packed[whole * count :, :] = jnp.concatenate([rows[0:half, rest:], rows[half:, rest:]], axis=1)


def unpack(packed, rows, at, count):
    width = rows.shape[1]
    whole = width // LANES
    for i in range(whole):
        rows[at : at + count, i * LANES : (i + 1) * LANES] = packed[i * count : (i + 1) * count, :]
    half = count // 2
    rest = whole * LANES
    rows[at : at + half, rest:] = packed[whole * count :, : width - rest]
    rows[at + half : at + count, rest:] = packed[whole * count :, width - rest :]


def pick_kernel(quarter, listed, own, core, new, piece, rows):
    blk = own.shape[1]
    part = new.shape[0] // 4
    ks = [quarter * quarter_of(0) + j for j in range(quarter)]
    fetch_blocks(listed, ks, own, core, rows)
    mine = pl.ds(pl.multiple_of(quarter_of(0) * part, part), part)
    rows[pl.ds(quarter * blk, part), :] = new[mine, :]
    pack(rows, piece)


def pick_quarter(listed, own, core, new, quarter):
    _, blk, width = own.shape
    rows = quarter * blk + new.shape[0] // 4
    return pl.pallas_call(
        functools.partial(pick_kernel, quarter),
        out_shape=in_vmem(packed_shape(rows, width)),
        in_specs=[SMEM_SPEC, VMEM_SPEC, VMEM_SPEC, VMEM_SPEC],
        out_specs=VMEM_SPEC,
        scratch_shapes=[pltpu.VMEM((rows, width), jnp.bfloat16)],
        compiler_params=pltpu.CompilerParams(vmem_limit_bytes=8 << 20),
        cost_estimate=pl.CostEstimate(
            flops=0, bytes_accessed=4 * quarter * blk * width, transcendentals=0
        ),
        name="pick_quarter",
    )(listed, *[pin(value, pltpu.VMEM) for value in (own, core, new)])


def attend_kernel(cfg, *refs):
    spans, sizes, pairs, groups, gather, turn, last, tokens, lat, items = cfg
    refs = list(refs)
    take = lambda n: [refs.pop(0) for _ in range(n)]
    (cached,) = take(1)
    listed, own, core = take(3) if gather else (None, None, None)
    (q,) = take(1)
    bufs = take(len(sizes))
    state_in = {}
    for group in groups:
        m_in, l_in, acc_in = take(3)
        for at, i in enumerate(group):
            state_in[i] = (m_in, l_in, acc_in, at)
    (to_turn,) = take(1) if turn else (None,)
    if last:
        uv, wo_hbm = take(2)
        ho_out, *sent = take(1 + len({part for part, *_ in items}))
    else:
        acc, m_ref, l_ref = take(3)
        kv_out, direct = take(2) if gather else (None, None)
        (turned,) = take(1) if turn else (None,)
    kv, vt, cap, s_buf, p_buf, sems = take(6)
    (far_rows,) = take(1) if gather else (None,)
    if last:
        ho_t, *weights = refs
    keys = kv.shape[0]

    hist = 0
    if gather:
        hist, blk = kv_out.shape[0], own.shape[1]
        fetch_blocks(listed, range(hist // blk), own, core, kv)
    weight_copies = start_weights(items, wo_hbm, weights, sems) if last else []

    at = 0
    for rows, is_new, limit_of in spans:
        limit = limit_of(cached[0])
        row = lax.broadcasted_iota(jnp.int32, (rows, tokens), 0)
        if is_new:
            limit = lax.broadcasted_iota(jnp.int32, (rows, tokens), 1) + 1 + limit
        cap[pl.ds(at, rows), :] = jnp.where(row < limit, pos_big, neg_big)
        at += rows
    at = hist
    for buf, (rows, packed) in zip(bufs, sizes):
        if packed:
            unpack(buf, kv, at, rows)
        else:
            kv[pl.ds(at, rows), :] = buf[...]
        at += rows
    if gather:
        for buf, size, start in ((kv, hist // 4, 0), (bufs[0], sizes[0][0] // 4, hist // 4)):
            rows = pl.ds(pl.multiple_of(quarter_of(3) * size, size), size)
            far_rows[pl.ds(start, size), :] = buf[rows, :]
        pack(far_rows, direct)
        kv_out[...] = kv[0:hist, :]

    def scores(n):
        i = pairs[n]
        q_pair = jnp.concatenate([q[2 * i], q[2 * i + 1]], axis=1)
        s_buf[n % 2] = jnp.dot(kv[...], q_pair, preferred_element_type=jnp.float32)

    def fold(x):
        return x.reshape(CHUNK // 8, 8, x.shape[1])

    scores(0)
    vt[...] = kv[:, :lat].T
    for n, i in enumerate(pairs):
        if n + 1 < len(pairs):
            scores(n + 1)
        buf, weight = s_buf.at[n % 2], p_buf.at[n % 2]
        top = jnp.full((8, 2 * tokens), -jnp.inf, jnp.float32)
        for r in range(0, keys, CHUNK):
            limits = cap[r : r + CHUNK, :]
            x = jnp.minimum(buf[r : r + CHUNK, :], jnp.concatenate([limits, limits], axis=1))
            top = jnp.maximum(top, jnp.max(fold(x), axis=0))
        m = jnp.max(top, axis=0, keepdims=True)
        if state_in:
            m_in, l_in, acc_in, at = state_in[i]
            m_old, l_old, acc_old = m_in[at], l_in[at], acc_in[at]
            m = jnp.maximum(m, m_old)
        scaled = m * exp2_scale
        total = jnp.zeros((8, 2 * tokens), jnp.float32)
        for r in range(0, keys, CHUNK):
            limits = cap[r : r + CHUNK, :]
            x = jnp.minimum(buf[r : r + CHUNK, :], jnp.concatenate([limits, limits], axis=1))
            p = jnp.exp2(x * exp2_scale - scaled)
            total = total + jnp.sum(fold(p), axis=0)
            weight[r : r + CHUNK, :] = p.astype(jnp.bfloat16)
        l = jnp.sum(total, axis=0, keepdims=True)
        o = jnp.dot(vt[...], weight[...], preferred_element_type=jnp.float32)
        if state_in:
            factor = jnp.exp2(m_old * exp2_scale - scaled)
            l = l + l_old * factor
            o = o + acc_old * factor
        if not last:
            m_ref[n] = m
            l_ref[n] = l
            acc[n] = o
            continue
        latent = (o * (1.0 / l)).astype(jnp.bfloat16)
        vh = uv.shape[1]
        both = uv[2 * i : 2 * i + 2].reshape(2 * vh, lat)
        out = jnp.dot(both, latent, preferred_element_type=jnp.float32).astype(jnp.bfloat16)
        for k in range(2):
            own_part = out[k * vh : (k + 1) * vh, k * tokens : (k + 1) * tokens]
            ho_t[pl.ds((2 * i + k) * vh, vh), :] = own_part
    if turn:
        for head in range(turned.shape[0]):
            turned[head] = to_turn[head].T
    if last:
        ho_out[...] = ho_t[...].T
        project_items(items, ho_out, weight_copies, weights, sent)


def start_weights(items, wo_hbm, weights, sems):
    copies, filled = [], {}
    parts = sorted({part for part, *_ in items})
    me = lax.axis_index("head")
    cols = wo_hbm.shape[1] // lax.axis_size("head")
    for n, (part, j, lo, width) in enumerate(items):
        at = filled.get(part, 0)
        filled[part] = at + width
        copies.append(
            pltpu.make_async_copy(
                wo_hbm.at[:, pl.ds(pl.multiple_of((me ^ j) * cols + lo, LANES), width)],
                weights[parts.index(part)].at[:, pl.ds(at, width)],
                sems.at[1 + n],
            )
        )
        copies[-1].start()
    return copies


def project_items(items, head_out, copies, weights, outs):
    parts = sorted({part for part, *_ in items})
    for n, part in enumerate(parts):
        widths = [width for other, _, _, width in items if other == part]
        for copy, (other, *_) in zip(copies, items):
            if other == part:
                copy.wait()
        value = jnp.dot(head_out[...], weights[n][...], preferred_element_type=jnp.float32)
        for at, width in enumerate(widths):
            outs[n][at] = value[:, at * width : (at + 1) * width].astype(jnp.bfloat16)


def weight_shapes(items, depth):
    sizes = {}
    for part, _, _, width in items:
        sizes[part] = sizes.get(part, 0) + width
    return [pltpu.VMEM((depth, sizes[part]), jnp.bfloat16) for part in sorted(sizes)]


def item_shapes(items, tokens):
    sizes = {}
    for part, _, _, size in items:
        sizes[part] = (sizes.get(part, (0, size))[0] + 1, size)
    return [in_vmem((sizes[part][0], tokens, sizes[part][1])) for part in sorted(sizes)]


def attend(spans, cached, q_t, bufs, pairs, state, lat, gather=None, turn=None, last=None):
    heads, width, tokens = q_t.shape
    items = last[2] if last else ()
    keys = sum(rows for rows, *_ in spans)
    stat = (len(pairs), 1, 2 * tokens)
    flops = 4 * len(pairs) * tokens * keys * (width + lat)
    moved = 2 * keys * width
    inputs, specs = [pin(cached, pltpu.SMEM)], [SMEM_SPEC]
    if gather:
        listed, own, core, hist = gather
        inputs += [listed, pin(own, pltpu.VMEM), pin(core, pltpu.VMEM)]
        specs += [SMEM_SPEC, VMEM_SPEC, VMEM_SPEC]
    vmem = [q_t, *bufs]
    for _, arrays in state:
        vmem += arrays
    if turn is not None:
        vmem.append(turn)
    scratch = [
        pltpu.VMEM((keys, width), jnp.bfloat16),
        pltpu.VMEM((lat, keys), jnp.bfloat16),
        pltpu.VMEM((keys, tokens), jnp.float32),
        pltpu.VMEM((2, keys, 2 * tokens), jnp.float32),
        pltpu.VMEM((2, keys, 2 * tokens), jnp.bfloat16),
        pltpu.SemaphoreType.DMA((1 + len(items),)),
    ]
    if gather:
        far = (hist + bufs[0].shape[0]) // 4
        scratch.append(pltpu.VMEM((far, width), jnp.bfloat16))
    if last:
        up, proj, _ = last
        vmem.append(up)
        out_shape = [in_vmem((tokens, heads * up.shape[1])), *item_shapes(items, tokens)]
        scratch.append(pltpu.VMEM((heads * up.shape[1], tokens), jnp.bfloat16))
        scratch += weight_shapes(items, proj.shape[0])
        columns = sum(size for _, _, _, size in items)
        flops += 2 * tokens * proj.shape[0] * columns
        moved += 2 * proj.shape[0] * columns
    else:
        out_shape = [
            in_vmem((len(pairs), lat, 2 * tokens), jnp.float32),
            in_vmem(stat, jnp.float32),
            in_vmem(stat, jnp.float32),
        ]
        if gather:
            out_shape += [in_vmem((hist, width)), in_vmem(packed_shape(far, width))]
        if turn is not None:
            out_shape.append(in_vmem((turn.shape[0], turn.shape[2], turn.shape[1])))
    inputs += [pin(value, pltpu.VMEM) for value in vmem]
    specs += [VMEM_SPEC] * len(vmem)
    if last:
        inputs.append(pin(proj, pltpu.HBM))
        specs.append(HBM_SPEC)
    groups = tuple(group for group, _ in state)
    sizes = tuple((buf.size // width, buf.shape[1] != width) for buf in bufs)
    cfg = (
        tuple(spans), sizes, pairs, groups, bool(gather), turn is not None, bool(last), tokens, lat,
        items,
    )
    outs = pl.pallas_call(
        functools.partial(attend_kernel, cfg),
        out_shape=out_shape,
        in_specs=specs,
        out_specs=[VMEM_SPEC] * len(out_shape),
        scratch_shapes=scratch,
        compiler_params=pltpu.CompilerParams(vmem_limit_bytes=24 << 20),
        cost_estimate=pl.CostEstimate(
            flops=flops, bytes_accessed=moved, transcendentals=2 * len(pairs) * tokens * keys
        ),
        name="attend_last" if last else "attend_gather" if gather else "attend",
    )(*inputs)
    return outs if last else ((pairs, (outs[1], outs[2], outs[0])), *outs[3:])


def project_kernel(items, head_out, wo_hbm, *refs):
    parts = len({part for part, *_ in items})
    outs, (sems, *weights) = refs[:parts], refs[parts:]
    copies = start_weights(items, wo_hbm, weights, sems)
    project_items(items, head_out, copies, weights, outs)


def project(head_out, proj, items, name):
    tokens, depth = head_out.shape
    out_shape = item_shapes(items, tokens)
    columns = sum(size for _, _, _, size in items)
    return pl.pallas_call(
        functools.partial(project_kernel, items),
        out_shape=out_shape,
        in_specs=[VMEM_SPEC, HBM_SPEC],
        out_specs=[VMEM_SPEC] * len(out_shape),
        scratch_shapes=[pltpu.SemaphoreType.DMA((1 + len(items),))]
        + weight_shapes(items, depth),
        compiler_params=pltpu.CompilerParams(vmem_limit_bytes=16 << 20),
        cost_estimate=pl.CostEstimate(
            flops=2 * tokens * depth * columns, bytes_accessed=2 * depth * columns, transcendentals=0
        ),
        name=name,
    )(pin(head_out, pltpu.VMEM), pin(proj, pltpu.HBM))


def flip_bit(value, axis, bit):
    size = lax.axis_size(axis)
    return lax.ppermute(value, axis, [(i, i ^ (1 << bit)) for i in range(size)])


def from_ahead(value, steps):
    size = lax.axis_size("ctx")
    return lax.ppermute(value, "ctx", [((i + steps) % size, i) for i in range(size)])


def add_halves(a, b):
    return (a.astype(jnp.float32) + b.astype(jnp.float32)).astype(jnp.bfloat16)


def sum_parts(kept, sent, orders):
    keeps, done, latest = list(kept), [None] * len(orders), None
    coming = [flip_bit(send, "head", order[0]) for send, order in zip(sent, orders)]
    for stage in range(len(orders[0])):
        for part, order in enumerate(orders):
            got, keep = coming[part], keeps[part]
            if latest is not None:
                got, _ = tie(got, latest)
            if stage + 1 == len(order):
                done[part] = keep[0].astype(jnp.float32) + got[0].astype(jnp.float32)
                continue
            half = keep.shape[0] // 2
            latest = add_halves(keep[half:], got[half:])
            coming[part] = flip_bit(latest, "head", order[stage + 1])
            keeps[part] = add_halves(keep[:half], got[:half])
    return done


def sum_to_owner(keep, send, order):
    for stage, bit in enumerate(order):
        got = flip_bit(send, "head", bit)
        if stage + 1 == len(order):
            return keep[0].astype(jnp.float32) + got[0].astype(jnp.float32)
        half = keep.shape[0] // 2
        send = add_halves(keep[half:], got[half:])
        keep = add_halves(keep[:half], got[:half])


def tie(*values):
    return lax.optimization_barrier(values)


def body(queries, new_latent, cache_pool, block_list, cached_lengths, w_uv, w_o):
    n_ctx = lax.axis_size("ctx")
    n_head = lax.axis_size("head")
    pool = cache_pool[0]
    slots, blk, width = pool.shape
    tokens = queries.shape[1]
    lat = w_uv.shape[1]
    blocks = block_list.shape[2]
    hist = blocks * blk
    part = hist // 4
    new_part = tokens // 4
    proj = w_o.reshape(w_o.shape[0] * w_o.shape[1], w_o.shape[2])
    q_t = jnp.transpose(queries[0], (1, 2, 0))
    cols = proj.shape[1] // n_head
    pairs = tuple(range(q_t.shape[0] // 2))
    pairs_a, pairs_b = pairs[: (len(pairs) + 1) // 2], pairs[(len(pairs) + 1) // 2 :]

    def source_of(step):
        return lax.rem(lax.axis_index("ctx") + step, n_ctx)

    def piece_spans(step, flip):
        def history(cached):
            return cached - source_of(step) * hist - part * quarter_of(flip)

        def new(cached):
            ahead = (lax.axis_index("ctx") - source_of(step)) * tokens
            return ahead - new_part * quarter_of(flip)

        return [(part, False, history), (new_part, True, new)]

    own_spans = [
        (hist, False, lambda cached: cached - lax.axis_index("ctx") * hist),
        (tokens, True, lambda cached: 0),
    ]

    core = flip_bit(pool, "pool", 0)
    own, new_own = stage(pool, jnp.transpose(new_latent[0], (1, 0)))
    listed = block_list[0, 0] - slots * lax.axis_index("pool")
    piece = pick_quarter(listed, own, core, new_own, blocks // 4)
    by_x = from_ahead(piece, 1)
    begun, kv_own, direct = attend(
        own_spans, cached_lengths, q_t, [new_own], pairs_a, [], lat, gather=(listed, own, core, hist)
    )
    by_x, direct, kv_own = tie(by_x, direct, kv_own)
    state = [begun]
    arrivals = []
    for step in range(1, n_ctx):
        if step > 1:
            by_x = from_ahead(piece, step)
        by_y = flip_bit(by_x, "head", 0)
        by_z = flip_bit(by_x, "head", 1)
        arrivals.append((by_x, by_y, by_z, from_ahead(direct, step)))
    if pairs_b:
        state += attend(own_spans, cached_lengths, q_t, [kv_own, new_own], pairs_b, [], lat)

    bits = n_head.bit_length() - 1
    half = n_head // 2
    if cols % LANES == 0 and n_head == 8:
        outer = 2 * cols // 7 // LANES * LANES
        orders = ((0, 1, 2), (1, 0, 2), (0, 1, 2))
        widths = (outer, cols - 2 * outer, outer)
        spans = [(sum(widths[:i]), widths[i]) for i in range(3)]
        ranked = [
            [(part, j, *spans[part]) for j in slot_order(order)] for part, order in enumerate(orders)
        ]
        early = tuple(ranked[0][half:] + ranked[1][half:])
        late = tuple(ranked[2][half:])
        keeps = tuple(item for ranks in ranked for item in ranks[:half])
    else:
        orders, early = (), ()

    up = None
    for step in range(1, n_ctx):
        by_x, *others = arrivals[step - 1]
        spans = piece_spans(step, 0)
        begun, *turned = attend(
            spans, cached_lengths, q_t, [by_x], pairs, state, lat, turn=w_uv if up is None else None
        )
        up = turned[0] if turned else up
        state = [begun]
        spans = piece_spans(step, 1) + piece_spans(step, 2) + piece_spans(step, 3)
        if step + 1 < n_ctx:
            state = attend(spans, cached_lengths, q_t, others, pairs, state, lat)
    head_out, *sent = attend(
        spans, cached_lengths, q_t, others, pairs, state, lat, last=(up, proj, early)
    )
    if orders:
        sent += project(head_out, proj, late, "project_late")
        head_out, sent[2] = tie(head_out, sent[2])
        kept = project(head_out, proj, keeps, "project_kept")
        done = sum_parts(kept, sent, orders)
        return jnp.concatenate(done, axis=1).astype(jnp.bfloat16)[None]
    partial_out = jnp.dot(head_out, proj, preferred_element_type=jnp.float32)
    blocks = jnp.transpose(partial_out.reshape(tokens, n_head, cols), (1, 0, 2)).astype(jnp.bfloat16)
    order = tuple(range(bits))
    mine = lax.axis_index("head") ^ jnp.array(slot_order(order), jnp.int32)
    blocks = jnp.take(blocks, mine, axis=0)
    return sum_to_owner(blocks[:half], blocks[half:], order).astype(jnp.bfloat16)[None]


def solution(mesh):
    in_specs = (
        P("pool", "ctx", "head", None),
        P("pool", "ctx", None),
        P("ctx", "pool", None, None),
        P("pool", "ctx", None),
        P("pool"),
        P("head", None, None),
        P("head", None, None),
    )
    out_specs = P("pool", "ctx", "head")
    return jax.shard_map(body, mesh=mesh, in_specs=in_specs, out_specs=out_specs, check_vma=False)
```
